128 devices in a mesh: sec: 8 (over z_hi, y), dev: 16 (over x, z_lo, core).
Axes of the slice: x: 4, y: 4, z: 4 (z_hi: 2, z_lo: 2; z = z_hi * 2 + z_lo), core: 2. Of those that a mesh axis runs over, the one named last changes fastest.
Arguments:
- child_panel: bfloat16 [8, 6144, 2048], P('sec', 'dev'), may hold values from -0.23925781 to 0.23925781
- child_inverse: bfloat16 [8, 2048, 2048], P('sec'), may hold values from -0.03756505 to 1.5, as said below
- child_map: int32 [8, 48], replicated, may hold values from 0 to 63, as said below
- parent_front: bfloat16 [8192, 8192], P('sec', 'dev'), may hold values from -6 to 6
- parent_inverse: bfloat16 [1024, 1024], replicated, may hold values from -0.00166015625 to 0.046875, as said below
- parent_pivots: int32 [8], replicated, may hold values from 0 to 63, as said below
Outputs:
- parent_update: float32 [8192, 8192], P('sec', 'dev')
- parent_factor: bfloat16 [8192, 1024], P('sec')
The draws below stay inside these ranges and needn't reach their ends.
Inputs may be any that keep to these rules, and one draw needn't show every extreme that they name: `child_map`: each row names 48 different parent blocks. `parent_pivots`: 8 different parent blocks. `child_inverse`: upper triangular with positive diagonal. `parent_inverse`: upper triangular with positive diagonal.
All inputs are finite; a program needn't handle non-finite values.
Results may differ from the reference program's by a relative error of at most 0.014.
Values may be sent and summed in bfloat16 or wider, within the bound.
No kernel may reach another device: no remote copies, remote signals or barrier semaphores. Data moves between devices by JAX's collectives and lax.ppermute only.
A program may use at most 128 MiB of HBM per device.

```python
import jax
import jax.numpy as jnp
from jax import lax

BLK = 128
PIV = 2048
CROWS = 6144
PORD = 8192
KP = 1024
CBLK = 48
PBLK = 64
KB = 8
N_SEC = 8


def upper_factor(key, order, diag_scale, off_scale):
    key_off, key_diag = jax.random.split(key, 2)
    off_part = jax.random.uniform(key_off, (order, order), jnp.float32, -1.6, 1.6) * off_scale
    diagonal = jax.random.uniform(key_diag, (order,), jnp.float32, 0.5, 1.45) * diag_scale
    return jnp.triu(off_part, 1) + jnp.diag(diagonal)


def spanning(key, count, total):
    key_rest, key_order = jax.random.split(key)
    middle = jax.random.permutation(key_rest, jnp.arange(1, total - 1, dtype=jnp.int32))[:count - 2]
    chosen = jnp.concatenate([jnp.array([0, total - 1], jnp.int32), middle])
    return jax.random.permutation(key_order, chosen)


def draw_child_inverse(key, part):
    keys = jax.random.split(jax.random.fold_in(key, 11), N_SEC)
    stacked = jax.vmap(lambda one_key: upper_factor(one_key, PIV, 1.0, PIV ** (-0.5)))(keys)
    return stacked.astype(jnp.bfloat16)


def draw_parent_inverse(key, part):
    return upper_factor(jax.random.fold_in(key, 13), KP, KP ** (-0.5), 1.0 / KP).astype(jnp.bfloat16)


def draw_child_map(key, part):
    keys = jax.random.split(jax.random.fold_in(key, 17), N_SEC)
    return jax.vmap(lambda one_key: spanning(one_key, CBLK, PBLK))(keys)


def draw_parent_pivots(key, part):
    return spanning(jax.random.fold_in(key, 19), KB, PBLK)


def block_scale(rng, extent, shards, smallest, largest):
    def one(dim, blocks):
        draws = jax.random.uniform(jax.random.fold_in(jax.random.fold_in(rng, 6), dim), (blocks,), jnp.float32, smallest / len(shards), largest / len(shards))
        return jnp.repeat(jnp.exp(draws), extent[dim] // blocks).reshape((-1,) + (1,) * (len(extent) - dim - 1))

    loudness = one(*shards[0])
    for cut in shards[1:]:
        loudness = loudness * one(*cut)
    return loudness


def gaussian(stream_key, dims, spread, most, shards=(), held_as=jnp.bfloat16):
    values = jax.random.normal(stream_key, dims, jnp.float32) * spread
    if len(shards) > 0:
        values = block_scale(stream_key, dims, shards, -0.22, 0.18) * values
    return jnp.clip(values, min=-most, max=most).astype(held_as)


def setup_inputs(seed: int = 0) -> dict:
    arg_keys = jax.random.split(jax.random.key(seed), 7)
    return {
        "child_panel": gaussian(arg_keys[0], (N_SEC, CROWS, PIV), 0.04, 0.23925781, ((0, 8), (1, 16))),
        "child_inverse": draw_child_inverse(jax.random.fold_in(arg_keys[6], 71), 0),
        "child_map": draw_child_map(jax.random.fold_in(arg_keys[6], 71), 0),
        "parent_front": gaussian(arg_keys[3], (PORD, PORD), 1.0, 6.0, ((0, 8), (1, 16))),
        "parent_inverse": draw_parent_inverse(jax.random.fold_in(arg_keys[6], 71), 0),
        "parent_pivots": draw_parent_pivots(jax.random.fold_in(arg_keys[6], 71), 0),
    }


def block_positions(blocks):
    offsets = jnp.arange(BLK, dtype=jnp.int32)
    return (blocks.astype(jnp.int32)[:, None] * BLK + offsets[None, :]).reshape(-1).astype(jnp.int32)


def product(left, right):
    return jnp.dot(left.astype(jnp.float32), right.astype(jnp.float32), precision=lax.Precision.HIGHEST)


def outer_rows(left_rows, right_rows):
    return lax.dot_general(left_rows.astype(jnp.float32), right_rows.astype(jnp.float32), (((1,), (1,)), ((), ())), precision=lax.Precision.HIGHEST)


def reference(child_panel, child_inverse, child_map, parent_front, parent_inverse, parent_pivots):
    summed_blocks = jnp.zeros((PBLK, BLK, PBLK, BLK), jnp.float32)
    for child_index in range(N_SEC):
        factor_rows = product(child_panel[child_index], child_inverse[child_index]).astype(jnp.bfloat16)
        contribution = (-outer_rows(factor_rows, factor_rows)).astype(jnp.bfloat16)
        pieces = contribution.astype(jnp.float32).reshape(CBLK, BLK, CBLK, BLK).transpose(0, 2, 1, 3)
        blocks = child_map[child_index].astype(jnp.int32)
        summed_blocks = summed_blocks.at[blocks[:, None], :, blocks[None, :], :].add(pieces)
    summed = summed_blocks.reshape(PORD, PORD)
    assembled = parent_front.astype(jnp.float32) + summed
    pivot_cols = block_positions(parent_pivots)
    panel_values = assembled[:, pivot_cols].astype(jnp.bfloat16)
    parent_factor = product(panel_values, parent_inverse).astype(jnp.bfloat16)
    is_pivot = jnp.zeros((PORD,), jnp.bool_).at[pivot_cols].set(True)
    trailing = jnp.where(is_pivot[:, None], jnp.zeros_like(parent_factor), parent_factor)
    parent_update = assembled - outer_rows(trailing, trailing)
    return parent_update, parent_factor
```

```python
import functools

import jax
import jax.numpy as jnp
from jax import lax
from jax.experimental import pallas as pl
from jax.experimental.pallas import tpu as pltpu
from jax.sharding import Mesh
from jax.sharding import PartitionSpec as P

BLK = 128
PORD = 8192
PIV = 2048
KH = PIV // 2
OWN = 384
BF = jnp.bfloat16
F32 = jnp.float32
SIZE = {"h": 2, "y": 4, "x": 4, "z": 2, "c": 2}
AXES = ("h", "y", "x", "z", "c")
KEYS = [(0, 0), (3, 0), (1, 0), (0, 1), (2, 0), (3, 1), (1, 1), (2, 1)]


def shift(array, axis, step):
    size = SIZE[axis]
    return lax.ppermute(array, axis, [(i, (i + step) % size) for i in range(size)])


def gather_rows(s0, s1):
    w0 = shift(s0, "x", 1)
    e0 = shift(s0, "x", -1)
    z0 = shift(s0, "z", 1)
    w1 = shift(s1, "x", 1)
    e1 = shift(s1, "x", -1)
    z1 = shift(s1, "z", 1)
    q0 = shift(w0, "x", 1)
    q1 = shift(e1, "x", -1)
    b0 = shift(z0, "x", 1)
    a1 = shift(z1, "x", -1)
    a0 = shift(e0, "z", 1)
    b1 = shift(w1, "z", 1)
    r0a = shift(b0[:256], "x", 1)
    r0b = shift(q0[256:], "z", 1)
    r1a = shift(a1[:256], "x", -1)
    r1b = shift(q1[256:], "z", 1)
    mine = {
        (0, 0): [[s0], [s1]],
        (3, 0): [[w0], [w1]],
        (1, 0): [[e0], [e1]],
        (0, 1): [[z0], [z1]],
        (2, 0): [[q0], [q1]],
        (3, 1): [[b0], [b1]],
        (1, 1): [[a0], [a1]],
        (2, 1): [[r0a, r0b], [r1a, r1b]],
    }
    other = {k: [[shift(p, "c", 1) for p in half] for half in v] for k, v in mine.items()}
    return mine, other


def piece_list(mine, other):
    out = []
    for place, key in enumerate(KEYS):
        for dc, table in enumerate((mine, other)):
            for half in range(2):
                row = (place * 2 + dc) * OWN
                for array in table[key][half]:
                    out.append((array, row, array.shape[0], half))
                    row += array.shape[0]
    return out


def contribution_kernel(pieces, n_main, dest, chosen, pan_rows, pan_cols, offset, *refs):
    n = len(pieces)
    ins = refs[:n]
    outs = refs[n : n + n_main]
    pans = refs[n + n_main : n + n_main + 8]
    rows, cols, placed, left, right, pan, sem_in, sem_sel, sem_out, sem_pan = refs[n + n_main + 8 :]

    def selection(m, start):
        for i, (first, count, half) in enumerate(pieces):
            for b in range(count // BLK):
                copy = pltpu.make_async_copy(
                    ins[i].at[pl.ds(b * BLK, BLK), :],
                    cols.at[pl.ds(m * BLK, BLK), pl.ds(half * KH, KH)],
                    sem_sel.at[m, half],
                )

                @pl.when(chosen[m] == first // BLK + b)
                def _(copy=copy):
                    copy.start()

    for m in range(4):
        selection(m, True)

    def arrival(i):
        first, count, half = pieces[i]
        return pltpu.make_async_copy(
            ins[i],
            rows.at[pl.ds(first, count), pl.ds(half * KH, KH)],
            sem_in.at[i],
        )

    for i in range(n):
        arrival(i).start()

    @pl.loop(0, PORD // BLK)
    def _(i):
        for half in range(2):
            placed[half, pl.ds(i * BLK, BLK), :] = jnp.zeros((BLK, 256), BF)

    for m in range(4):

        @pl.when(chosen[m] < 0)
        def _(m=m):
            cols[pl.ds(m * BLK, BLK), :] = jnp.zeros((BLK, PIV), BF)

        @pl.when(chosen[m] >= 0)
        def _(m=m):
            for half in range(2):
                pltpu.make_async_copy(
                    ins[0].at[pl.ds(0, BLK), :],
                    cols.at[pl.ds(m * BLK, BLK), pl.ds(half * KH, KH)],
                    sem_sel.at[m, half],
                ).wait()

    done = 0
    for chunk in range(8):
        while done < n and pieces[done][0] < (chunk + 1) * 768:
            arrival(done).wait()
            done += 1

        @pl.loop(0, 2)
        def _(part, chunk=chunk):
            base = chunk * 6 + part * 3
            product = lax.dot_general(
                rows[pl.ds(base * BLK, OWN), :],
                cols[...],
                (((1,), (1,)), ((), ())),
                preferred_element_type=F32,
            )
            for b in range(3):
                block = (-product[b * BLK : (b + 1) * BLK]).astype(BF)
                at = pl.multiple_of(dest[base + b] * BLK, BLK)
                placed[0, pl.ds(at, BLK), :] = block[:, :256]
                placed[1, pl.ds(at, BLK), :] = block[:, 256:]

    def leaving(i):
        return pltpu.make_async_copy(
            placed.at[i % 2, pl.ds((i // 2) * 1024, 1024), :], outs[i], sem_out.at[i]
        )

    for i in range(n_main):
        leaving(i).start()

    for q in range(8):

        @pl.when(pan_rows[q] < 0)
        def _(q=q):
            left[pl.ds(q * 64, 64), :] = jnp.zeros((64, PIV), BF)

        @pl.when(pan_rows[q] >= 0)
        def _(q=q):
            at = pl.multiple_of(pan_rows[q] * BLK + offset[0], 64)
            left[pl.ds(q * 64, 64), :] = rows[pl.ds(at, 64), :]

        @pl.when(pan_cols[q] < 0)
        def _(q=q):
            right[pl.ds(q * BLK, BLK), :] = jnp.zeros((BLK, PIV), BF)

        @pl.when(pan_cols[q] >= 0)
        def _(q=q):
            at = pl.multiple_of(pan_cols[q] * BLK, BLK)
            right[pl.ds(q * BLK, BLK), :] = rows[pl.ds(at, BLK), :]

    @pl.loop(0, 2)
    def _(half):
        pan[half] = (
            -lax.dot_general(
                left[...],
                right[pl.ds(pl.multiple_of(half * 512, 512), 512), :],
                (((1,), (1,)), ((), ())),
                preferred_element_type=F32,
            )
        ).astype(BF)

    def pan_leaving(i):
        return pltpu.make_async_copy(
            pan.at[i % 2, pl.ds((i // 2) * 128, 128), :], pans[i], sem_pan.at[i]
        )

    for i in range(8):
        pan_leaving(i).start()
    for i in range(8):
        pan_leaving(i).wait()
    for i in range(n_main):
        leaving(i).wait()


def contributions(pieces, dest, chosen, pan_rows, pan_cols, offset):
    arrays = [p[0] for p in pieces]
    spec = [p[1:] for p in pieces]
    n = len(arrays)
    any_space = pl.BlockSpec(memory_space=pl.ANY)
    results = pl.pallas_call(
        functools.partial(contribution_kernel, spec, 16),
        out_shape=[jax.ShapeDtypeStruct((1024, 256), BF)] * 16
        + [jax.ShapeDtypeStruct((128, 512), BF)] * 8,
        in_specs=[pl.BlockSpec(memory_space=pltpu.SMEM)] * 5 + [any_space] * n,
        out_specs=[any_space] * 24,
        scratch_shapes=[
            pltpu.VMEM((6144, PIV), BF),
            pltpu.VMEM((512, PIV), BF),
            pltpu.VMEM((2, PORD, 256), BF),
            pltpu.VMEM((512, PIV), BF),
            pltpu.VMEM((1024, PIV), BF),
            pltpu.VMEM((2, 512, 512), BF),
            pltpu.SemaphoreType.DMA((n,)),
            pltpu.SemaphoreType.DMA((4, 2)),
            pltpu.SemaphoreType.DMA((16,)),
            pltpu.SemaphoreType.DMA((8,)),
        ],
        compiler_params=pltpu.CompilerParams(vmem_limit_bytes=60 * 2**20),
        cost_estimate=pl.CostEstimate(
            flops=15_000_000_000, bytes_accessed=36_000_000, transcendentals=0
        ),
    )(dest, chosen, pan_rows, pan_cols, offset, *arrays)
    main, pan = results[:16], results[16:]
    main = [[[main[(dh * 4 + dy) * 2 + half] for half in range(2)] for dy in range(4)] for dh in range(2)]
    pan = [[pan[dy * 2 + half] for half in range(2)] for dy in range(4)]
    return main, pan


def ring_sum(parts):
    a = shift(parts[2][0], "y", 1)
    b = shift(parts[2][1], "y", -1)
    d1 = shift(parts[1][1], "y", 1)
    d0 = shift(parts[3][0], "y", -1)
    e0 = shift(parts[1][0] + a, "y", 1)
    e1 = shift(parts[3][1] + b, "y", -1)
    return [
        parts[0][0].astype(F32) + d0.astype(F32) + e0.astype(F32),
        parts[0][1].astype(F32) + d1.astype(F32) + e1.astype(F32),
    ]


def pick(bit, when_zero, when_one):
    return jnp.where(bit == 0, when_zero, when_one)


def ordered_pair(bit, own, other):
    return jnp.stack([pick(bit, own, other), pick(bit, other, own)])


def ordered_ring(at, parts):
    twice = jnp.stack(list(parts) + list(parts))
    return lax.dynamic_slice_in_dim(twice, (4 - at) % 4, 4, 0)


def front_panel(picked, x, z, c):
    v = picked.reshape(4, 2, 2, 64, 1024)
    v = pick(c, v[:, :, 0], v[:, :, 1]) + shift(pick(c, v[:, :, 1], v[:, :, 0]), "c", 1)
    own = lambda k: lax.dynamic_index_in_dim(v, (x + k) % 4, 0, keepdims=False)
    v = own(0) + shift(own(1), "x", 1) + shift(own(3), "x", -1) + shift(own(2), "x", 2)
    return pick(z, v[0], v[1]) + shift(pick(z, v[1], v[0]), "z", 1)


def local(child_panel, child_inverse, child_map, parent_front, parent_inverse, parent_pivots):
    h, y, x, z, c = (lax.axis_index(a) for a in AXES)
    sec = h * 4 + y
    dev = x * 4 + z * 2 + c

    my_map = lax.dynamic_index_in_dim(child_map, sec, 0, keepdims=False)
    place_of = {key: i for i, key in enumerate(KEYS)}
    place_table = jnp.array([[place_of[(dx, dz)] for dz in range(2)] for dx in range(4)], jnp.int32)
    child = jnp.arange(48, dtype=jnp.int32)
    owner = child // 3
    place = place_table[(owner // 4 - x) % 4, (owner // 2 % 2) ^ z]
    position = (place * 2 + ((owner % 2) ^ c)) * 3 + child % 3
    parent_row = my_map // 8
    slot = (((parent_row // 4) ^ h) * 4 + (parent_row % 4 - y) % 4) * 8 + my_map % 8
    dest = jnp.sum(
        jnp.where(position[None, :] == child[:, None], slot[None, :], 0), axis=1, dtype=jnp.int32
    )

    def find(targets):
        hit = my_map[None, :] == targets[:, None]
        return jnp.sum(jnp.where(hit, position[None, :] + 1, 0), axis=1, dtype=jnp.int32) - 1

    chosen = find(dev * 4 + jnp.arange(4, dtype=jnp.int32))
    slots = jnp.arange(8, dtype=jnp.int32)
    row_sec = ((slots % 2) ^ h) * 4 + (slots // 2 + y) % 4
    pan_rows = find(row_sec * 8 + dev // 2)
    pan_cols = find(parent_pivots)
    offset = (dev % 2 * 64).astype(jnp.int32).reshape(1)

    panel = child_panel[0]
    inverse = child_inverse[0]
    s0 = jnp.dot(panel[:, :KH], inverse[:KH, :KH], preferred_element_type=F32).astype(BF)
    s1 = jnp.dot(panel, inverse[:, KH:], preferred_element_type=F32).astype(BF)
    mine, other = gather_rows(s0, s1)

    main, pan = contributions(piece_list(mine, other), dest, chosen, pan_rows, pan_cols, offset)

    targets = dev * 4 + jnp.arange(4, dtype=jnp.int32)
    hot = (parent_pivots[:, None] == targets[None, :]).astype(BF)
    picked = jnp.einsum(
        "nri,pr->npi", parent_front.reshape(1024, 4, BLK), hot, preferred_element_type=F32
    ).astype(BF)
    front_rows = front_panel(picked.reshape(1024, 1024), x, z, c)

    pan_sum = ring_sum(pan)
    pan_sum = jnp.concatenate(pan_sum, axis=1)
    from_h = shift(pan_sum[64:].astype(BF), "h", 1)
    pan_rows_f = pan_sum[:64] + from_h.astype(F32) + front_rows.astype(F32)
    share = jnp.dot(pan_rows_f.astype(BF), parent_inverse, preferred_element_type=F32).astype(BF)

    row_block = sec * 8 + dev // 2
    masked = jnp.where(jnp.any(parent_pivots == row_block), jnp.zeros_like(share), share)
    pairs = [(s * 16 + d, (d % 8) * 16 + 2 * s + d // 8) for s in range(8) for d in range(16)]
    moved = lax.ppermute(masked, AXES, pairs)
    both = ordered_pair(h, moved, shift(moved, "h", 1))
    ring = ordered_ring(y, [both, shift(both, "y", -1), shift(both, "y", 2), shift(both, "y", 1)])
    column_factor = ring.transpose(1, 0, 2, 3).reshape(512, 1024)

    both = ordered_pair(z, share, shift(share, "z", 1))
    ring = ordered_ring(x, [both, shift(both, "x", -1), shift(both, "x", 2), shift(both, "x", 1)])
    both = ordered_pair(c, ring, shift(ring, "c", 1))
    parent_factor = both.transpose(1, 2, 0, 3, 4).reshape(1024, 1024)

    far = jnp.concatenate(ring_sum(main[1]), axis=1).astype(BF)
    far = shift(far, "h", 1)
    near = jnp.concatenate(ring_sum(main[0]), axis=1)
    assembled = parent_front.astype(F32) + near + far.astype(F32)

    my_blocks = sec * 8 + jnp.arange(8, dtype=jnp.int32)
    is_pivot = jnp.any(parent_pivots[None, :] == my_blocks[:, None], axis=1)
    row_pivot = jnp.repeat(is_pivot, BLK)
    trailing = jnp.where(row_pivot[:, None], jnp.zeros_like(parent_factor), parent_factor)
    update = lax.dot_general(
        trailing, column_factor, (((1,), (1,)), ((), ())), preferred_element_type=F32
    )
    return assembled - update, parent_factor


def solution(mesh):
    fine = Mesh(mesh.devices.reshape(tuple(SIZE[a] for a in AXES)), AXES)
    sec, dev = ("h", "y"), ("x", "z", "c")
    placed = (P(sec, dev, None), P(sec, None, None), P(), P(sec, dev), P(), P())
    return jax.shard_map(
        local,
        mesh=fine,
        in_specs=placed,
        out_specs=(P(sec, dev), P(sec, None)),
        check_vma=False,
    )
```

```python
import functools

import jax
import jax.numpy as jnp
from jax import lax
from jax.experimental import pallas as pl
from jax.experimental.pallas import tpu as pltpu
from jax.sharding import Mesh
from jax.sharding import PartitionSpec as P

BLK = 128
PORD = 8192
PIV = 2048
KH = PIV // 2
OWN = 384
STEP = 6
BF = jnp.bfloat16
F32 = jnp.float32
VMEM_LIMIT = 60 * 2**20
SMEM_SPEC = pl.BlockSpec(memory_space=pltpu.SMEM)
ANY_SPEC = pl.BlockSpec(memory_space=pl.ANY)
SIZE = {"h": 2, "y": 4, "x": 4, "z": 2, "c": 2}
AXES = ("h", "y", "x", "z", "c")
def shift(array, axis, step):
    size = SIZE[axis]
    return lax.ppermute(array, axis, [(i, (i + step) % size) for i in range(size)])


def mirrored(array, axis, step):
    size = SIZE[axis]
    pairs = [
        (i * 2 + core, (i + (step if core == 0 else -step)) % size * 2 + core)
        for i in range(size)
        for core in range(2)
    ]
    return lax.ppermute(array, (axis, "c"), pairs)


def after(value, *earlier):
    return lax.optimization_barrier((value,) + earlier)[0]


def factor_kernel(panel, inverse, out, held, sems):
    width = 512
    for j in range(PIV // width):
        deep = (j + 1) * width
        pltpu.make_async_copy(
            inverse.at[0, pl.ds(0, deep), pl.ds(j * width, width)],
            held.at[pl.ds(0, deep), pl.ds(j * width, width)],
            sems.at[j],
        ).start()
    for j in range(PIV // width):
        deep = (j + 1) * width
        pltpu.make_async_copy(
            inverse.at[0, pl.ds(0, deep), pl.ds(j * width, width)],
            held.at[pl.ds(0, deep), pl.ds(j * width, width)],
            sems.at[j],
        ).wait()
        out[:, j * width : deep] = jnp.dot(
            panel[0, :, :deep], held[:deep, j * width : deep], preferred_element_type=F32
        ).astype(BF)


def factor(panel, inverse):
    vmem = pl.BlockSpec(memory_space=pltpu.VMEM)
    return pl.pallas_call(
        factor_kernel,
        out_shape=jax.ShapeDtypeStruct((OWN, PIV), BF),
        in_specs=[vmem, ANY_SPEC],
        out_specs=vmem,
        scratch_shapes=[pltpu.VMEM((PIV, PIV), BF), pltpu.SemaphoreType.DMA((4,))],
        compiler_params=pltpu.CompilerParams(vmem_limit_bytes=VMEM_LIMIT),
        cost_estimate=pl.CostEstimate(
            flops=2_000_000_000, bytes_accessed=8_000_000, transcendentals=0
        ),
    )(panel, inverse)


def gather_rows(own, ready):
    w = mirrored(own, "x", 1)
    e = mirrored(own, "x", -1)
    z = shift(own, "z", 1)
    w, e, z, ready = lax.optimization_barrier((w, e, z, ready))
    core = shift(after(own, w), "c", 1)
    b = shift(w, "z", 1)
    q = mirrored(w, "x", 1)
    a = mirrored(z, "x", -1)
    core1 = shift(jnp.concatenate([after(w, core), e, z]), "c", 1)
    r = mirrored(b, "x", 1)
    last = [shift(v, "c", 1) for v in (q, a, b, r)]
    pieces, first = [], 0
    for array in (own, w, e, z, q, a, b, r, core, core1, *last):
        pieces.append((array, first, array.shape[0] // BLK))
        first += array.shape[0] // BLK
    return pieces, ready


PLACE = [[0, 3], [2, 5], [4, 7], [1, 6]]


def fetch(ins, pieces, block, dst, sem, first_row=0, count=BLK):
    for ref, (first, blocks) in zip(ins, pieces):

        @pl.when((block >= first) & (block < first + blocks))
        def _(ref=ref, first=first):
            row = pl.multiple_of((block - first) * BLK + first_row, 64)
            pltpu.make_async_copy(ref.at[pl.ds(row, count), :], dst, sem).start()


def fetched(ins, block, dst, sem, count=BLK):
    @pl.when(block < 0)
    def _():
        dst[...] = jnp.zeros((count, PIV), BF)

    @pl.when(block >= 0)
    def _():
        pltpu.make_async_copy(ins[0].at[pl.ds(0, count), :], dst, sem).wait()


def main_kernel(pieces, dest, chosen, *refs):
    n = len(pieces)
    ins, outs = refs[:n], refs[n : n + 16]
    rows, cols, placed, sem_in, sem_sel, sem_out = refs[n + 16 :]

    for m in range(4):
        fetch(ins, pieces, chosen[m], cols.at[pl.ds(m * BLK, BLK), :], sem_sel.at[m])

    def arrival(i):
        first, blocks = pieces[i]
        return pltpu.make_async_copy(
            ins[i], rows.at[pl.ds(first * BLK, blocks * BLK), :], sem_in.at[i]
        )

    for i in range(n):
        arrival(i).start()

    @pl.loop(0, PORD // 256)
    def _(i):
        for half in range(2):
            placed[half, pl.ds(pl.multiple_of(i * 256, 256), 256), :] = jnp.zeros((256, 256), BF)

    for m in range(4):
        fetched(ins, chosen[m], cols.at[pl.ds(m * BLK, BLK), :], sem_sel.at[m])

    def multiply(block, count):
        product = lax.dot_general(
            rows[pl.ds(block * BLK, count * BLK), :],
            cols[...],
            (((1,), (1,)), ((), ())),
            preferred_element_type=F32,
        )
        for b in range(count):
            at = pl.multiple_of(dest[block + b] * BLK, BLK)
            result = (-product[b * BLK : (b + 1) * BLK]).astype(BF)
            placed[0, pl.ds(at, BLK), :] = result[:, :256]
            placed[1, pl.ds(at, BLK), :] = result[:, 256:]

    done, at = 0, 0
    for i in range(n):
        arrival(i).wait()
        done += pieces[i][1]
        if (done - at) % STEP == 0:

            @pl.loop(0, (done - at) // STEP)
            def _(k, at=at):
                multiply(at + k * STEP, STEP)

            at = done

    def leaving(i):
        return pltpu.make_async_copy(
            placed.at[i % 2, pl.ds((i // 2) * 1024, 1024), :], outs[i], sem_out.at[i]
        )

    for i in range(16):
        leaving(i).start()
    for i in range(16):
        leaving(i).wait()


def main_parts(pieces, dest, chosen):
    arrays = [p[0] for p in pieces]
    n = len(arrays)
    outs = pl.pallas_call(
        functools.partial(main_kernel, [p[1:] for p in pieces]),
        out_shape=[jax.ShapeDtypeStruct((1024, 256), BF)] * 16,
        in_specs=[SMEM_SPEC] * 2 + [ANY_SPEC] * n,
        out_specs=[ANY_SPEC] * 16,
        scratch_shapes=[
            pltpu.VMEM((6144, PIV), BF),
            pltpu.VMEM((512, PIV), BF),
            pltpu.VMEM((2, PORD, 256), BF),
            pltpu.SemaphoreType.DMA((n,)),
            pltpu.SemaphoreType.DMA((4,)),
            pltpu.SemaphoreType.DMA((16,)),
        ],
        compiler_params=pltpu.CompilerParams(vmem_limit_bytes=VMEM_LIMIT),
        cost_estimate=pl.CostEstimate(
            flops=20_000_000_000, bytes_accessed=36_000_000, transcendentals=0
        ),
    )(dest, chosen, *arrays)
    return [[[outs[(dh * 4 + dy) * 2 + k] for k in range(2)] for dy in range(4)] for dh in range(2)]


def panel_kernel(pieces, pan_rows, pan_cols, offset, *refs):
    n = len(pieces)
    ins, out = refs[:n], refs[n]
    left, right, sem_left, sem_right = refs[n + 1 :]
    to_left = lambda q: left.at[pl.ds(q * 64, 64), :]
    to_right = lambda q: right.at[pl.ds(q * BLK, BLK), :]
    for q in range(8):
        fetch(ins, pieces, pan_rows[q], to_left(q), sem_left.at[q], offset[0], 64)
        fetch(ins, pieces, pan_cols[q], to_right(q), sem_right.at[q])
    for q in range(8):
        fetched(ins, pan_rows[q], to_left(q), sem_left.at[q], 64)
    for q in range(8):
        fetched(ins, pan_cols[q], to_right(q), sem_right.at[q])

    for part in range(4):
        product = lax.dot_general(
            left[...],
            right[pl.ds(part * 256, 256), :],
            (((1,), (1,)), ((), ())),
            preferred_element_type=F32,
        )
        out[:, part * 256 : (part + 1) * 256] = (-product).astype(BF)


def panel_parts(pieces, pan_rows, pan_cols, offset):
    arrays = [p[0] for p in pieces]
    n = len(arrays)
    return pl.pallas_call(
        functools.partial(panel_kernel, [p[1:] for p in pieces]),
        out_shape=jax.ShapeDtypeStruct((512, 1024), BF),
        in_specs=[SMEM_SPEC] * 3 + [ANY_SPEC] * n,
        out_specs=pl.BlockSpec(memory_space=pltpu.VMEM),
        scratch_shapes=[
            pltpu.VMEM((512, PIV), BF),
            pltpu.VMEM((1024, PIV), BF),
            pltpu.SemaphoreType.DMA((8,)),
            pltpu.SemaphoreType.DMA((8,)),
        ],
        compiler_params=pltpu.CompilerParams(vmem_limit_bytes=VMEM_LIMIT),
        cost_estimate=pl.CostEstimate(
            flops=2_200_000_000, bytes_accessed=8_000_000, transcendentals=0
        ),
    )(pan_rows, pan_cols, offset, *arrays)


def ring_sum(first, second):
    rings = (first, second)
    carried = [parts[3] for parts in rings]
    marks = []
    for k in (2, 1, 0):
        moved = [mirrored(v, "y", 1) for v in carried]
        marks.append(moved)
        carried = [parts[k].astype(F32) + v.astype(F32) for parts, v in zip(rings, moved)]
        if k > 0:
            carried = [v.astype(BF) for v in carried]
    return carried, marks


def pick(bit, when_zero, when_one):
    return jnp.where(bit == 0, when_zero, when_one)


def ordered_pair(bit, own, other):
    return jnp.stack([pick(bit, own, other), pick(bit, other, own)])


def ordered_ring(at, parts):
    twice = jnp.stack(list(parts) + list(parts))
    return lax.dynamic_slice_in_dim(twice, (4 - at) % 4, 4, 0)


def front_kernel(pivots, place, front, keep, send, zeros, sems):
    zeros[...] = jnp.zeros_like(zeros)
    for r in range(8):
        columns = pl.ds(r * BLK, BLK)
        local_block = pivots[r] - place[0] * 4
        mine = (local_block >= 0) & (local_block < 4)
        for k, out in enumerate((keep, send)):

            @pl.when(mine)
            def _(k=k, out=out, columns=columns, r=r):
                pltpu.make_async_copy(
                    front.at[:, place[1] ^ k, :, pl.ds(pl.multiple_of(local_block * BLK, BLK), BLK)],
                    out.at[:, :, columns],
                    sems.at[r, k],
                ).start()

            @pl.when(jnp.logical_not(mine))
            def _(k=k, out=out, columns=columns, r=r):
                pltpu.make_async_copy(zeros, out.at[:, :, columns], sems.at[r, k]).start()

    for r in range(8):
        for k, out in enumerate((keep, send)):
            pltpu.make_async_copy(zeros, out.at[:, :, pl.ds(r * BLK, BLK)], sems.at[r, k]).wait()


def front_pick(pivots, place, front):
    return pl.pallas_call(
        front_kernel,
        out_shape=[jax.ShapeDtypeStruct((8, 64, 1024), BF)] * 2,
        in_specs=[SMEM_SPEC] * 2 + [ANY_SPEC],
        out_specs=[ANY_SPEC] * 2,
        scratch_shapes=[pltpu.VMEM((8, 64, BLK), BF), pltpu.SemaphoreType.DMA((8, 2))],
        compiler_params=pltpu.CompilerParams(vmem_limit_bytes=VMEM_LIMIT),
    )(pivots, place, front.reshape(8, 2, 64, 512))


def local(child_panel, child_inverse, child_map, parent_front, parent_inverse, parent_pivots):
    h, y, x, z, c = (lax.axis_index(a) for a in AXES)
    sec = h * 4 + y
    dev = x * 4 + z * 2 + c

    my_map = lax.dynamic_index_in_dim(child_map, sec, 0, keepdims=False)
    place_table = jnp.array(PLACE, jnp.int32)
    child = jnp.arange(48, dtype=jnp.int32)
    owner = child // 3
    place = place_table[
        (owner // 4 - x) * (1 - 2 * (owner % 2)) % 4, (owner // 2 % 2) ^ z
    ]
    position = ((owner % 2) ^ c) * 24 + place * 3 + child % 3
    parent_row = my_map // 8
    slot = (((parent_row // 4) ^ h) * 4 + (parent_row % 4 - y) * (1 - 2 * c) % 4) * 8 + my_map % 8
    dest = jnp.sum(
        jnp.where(position[None, :] == child[:, None], slot[None, :], 0), axis=1, dtype=jnp.int32
    )

    def find(targets):
        hit = my_map[None, :] == targets[:, None]
        return jnp.sum(jnp.where(hit, position[None, :] + 1, 0), axis=1, dtype=jnp.int32) - 1

    chosen = find(dev * 4 + jnp.arange(4, dtype=jnp.int32))
    pan_rows = find(jnp.arange(8, dtype=jnp.int32) * 8 + dev // 2)
    pan_cols = find(parent_pivots)
    offset = (dev % 2 * 64).astype(jnp.int32).reshape(1)

    keep, send = front_pick(parent_pivots, jnp.stack([dev, c]).astype(jnp.int32), parent_front)
    front = (keep + shift(send, "c", 1)).reshape(4, 2, 64, 1024)
    front_x = [lax.dynamic_index_in_dim(front, (x + k) % 4, 0, keepdims=False) for k in range(4)]

    pieces, ready = gather_rows(
        factor(child_panel, child_inverse), (dest, chosen, pan_rows, pan_cols, offset, front_x)
    )
    dest, chosen, pan_rows, pan_cols, offset, front_x = ready

    pan = panel_parts(pieces, pan_rows, pan_cols, offset)
    arrived = lax.all_to_all(
        pan.reshape(8, 64, 1024), ("h", "y"), split_axis=0, concat_axis=0, tiled=True
    )
    main = main_parts(pieces, dest, chosen)

    front_x = [after(v, pan) for v in front_x]
    front_z = (
        front_x[0]
        + shift(front_x[1], "x", 1)
        + shift(front_x[3], "x", -1)
        + shift(front_x[2], "x", 2)
    )
    front_rows = pick(z, front_z[0], front_z[1]) + shift(pick(z, front_z[1], front_z[0]), "z", 1)

    arrived, main = lax.optimization_barrier((arrived, main))
    pan_rows_f = arrived.astype(F32).sum(axis=0) + front_rows.astype(F32)
    share = jnp.dot(pan_rows_f.astype(BF), parent_inverse, preferred_element_type=F32).astype(BF)

    far_in, near_in = ([[part[k] for part in main[d]] for k in range(2)] for d in (1, 0))
    far, marks = ring_sum(*far_in)
    near_in = [parts[:3] + [after(parts[3], mark)] for parts, mark in zip(near_in, marks[0])]
    far = [shift(v.astype(BF), "h", 1).astype(F32) for v in far]
    near, _ = ring_sum(*near_in)
    near = jnp.concatenate([n + f for n, f in zip(near, far)], axis=1)
    assembled = parent_front.astype(F32) + near

    row_block = sec * 8 + dev // 2
    masked = jnp.where(jnp.any(parent_pivots == row_block), jnp.zeros_like(share), share)
    masked = after(masked, marks[0][0])
    pairs = [(s * 16 + d, (d % 8) * 16 + 2 * s + d // 8) for s in range(8) for d in range(16)]
    moved = lax.ppermute(masked, AXES, pairs)
    ring = ordered_ring(y, [moved, shift(moved, "y", -1), shift(moved, "y", 2), shift(moved, "y", 1)])
    column_factor = ordered_pair(h, ring, shift(ring, "h", 1)).reshape(512, 1024)

    parent_factor = lax.all_gather(share, ("x", "z", "c"), axis=0, tiled=True)

    my_blocks = sec * 8 + jnp.arange(8, dtype=jnp.int32)
    is_pivot = jnp.any(parent_pivots[None, :] == my_blocks[:, None], axis=1)
    row_pivot = jnp.repeat(is_pivot, BLK)
    trailing = jnp.where(row_pivot[:, None], jnp.zeros_like(parent_factor), parent_factor)
    update = lax.dot_general(
        trailing, column_factor, (((1,), (1,)), ((), ())), preferred_element_type=F32
    )
    return assembled - update, parent_factor


def solution(mesh):
    fine = Mesh(mesh.devices.reshape(tuple(SIZE[a] for a in AXES)), AXES)
    sec, dev = ("h", "y"), ("x", "z", "c")
    placed = (P(sec, dev, None), P(sec, None, None), P(), P(sec, dev), P(), P())
    return jax.shard_map(
        local,
        mesh=fine,
        in_specs=placed,
        out_specs=(P(sec, dev), P(sec, None)),
        check_vma=False,
    )
```

```python
import functools

import jax
import jax.numpy as jnp
from jax import lax
from jax.experimental import pallas as pl
from jax.experimental.pallas import tpu as pltpu
from jax.sharding import Mesh
from jax.sharding import PartitionSpec as P

BLK = 128
PORD = 8192
PIV = 2048
KH = PIV // 2
OWN = 384
STEP = 12
BF = jnp.bfloat16
F32 = jnp.float32
VMEM_LIMIT = 60 * 2**20
SMEM_SPEC = pl.BlockSpec(memory_space=pltpu.SMEM)
ANY_SPEC = pl.BlockSpec(memory_space=pl.ANY)
SIZE = {"h": 2, "y": 4, "x": 4, "z": 2, "c": 2}
AXES = ("h", "y", "x", "z", "c")
def shift(array, axis, step):
    size = SIZE[axis]
    return lax.ppermute(array, axis, [(i, (i + step) % size) for i in range(size)])


def mirrored(array, axis, step):
    size = SIZE[axis]
    pairs = [
        (i * 2 + core, (i + (step if core == 0 else -step)) % size * 2 + core)
        for i in range(size)
        for core in range(2)
    ]
    return lax.ppermute(array, (axis, "c"), pairs)


def after(value, *earlier):
    return lax.optimization_barrier((value,) + earlier)[0]


def factor_kernel(panel, inverse, out, held, sems):
    width = 512
    for j in range(PIV // width):
        deep = (j + 1) * width
        pltpu.make_async_copy(
            inverse.at[0, pl.ds(0, deep), pl.ds(j * width, width)],
            held.at[pl.ds(0, deep), pl.ds(j * width, width)],
            sems.at[j],
        ).start()
    for j in range(PIV // width):
        deep = (j + 1) * width
        pltpu.make_async_copy(
            inverse.at[0, pl.ds(0, deep), pl.ds(j * width, width)],
            held.at[pl.ds(0, deep), pl.ds(j * width, width)],
            sems.at[j],
        ).wait()
        out[:, j * width : deep] = jnp.dot(
            panel[0, :, :deep], held[:deep, j * width : deep], preferred_element_type=F32
        ).astype(BF)


def factor(panel, inverse):
    vmem = pl.BlockSpec(memory_space=pltpu.VMEM)
    return pl.pallas_call(
        factor_kernel,
        out_shape=jax.ShapeDtypeStruct((OWN, PIV), BF),
        in_specs=[vmem, ANY_SPEC],
        out_specs=vmem,
        scratch_shapes=[pltpu.VMEM((PIV, PIV), BF), pltpu.SemaphoreType.DMA((4,))],
        compiler_params=pltpu.CompilerParams(vmem_limit_bytes=VMEM_LIMIT),
        cost_estimate=pl.CostEstimate(
            flops=2_000_000_000, bytes_accessed=8_000_000, transcendentals=0
        ),
    )(panel, inverse)


def gather_rows(own, ready):
    w = mirrored(own, "x", 1)
    e = mirrored(own, "x", -1)
    z = shift(own, "z", 1)
    core = shift(own, "c", 1)
    w, e, z, core, ready = lax.optimization_barrier((w, e, z, core, ready))
    b = shift(w, "z", 1)
    q = mirrored(w, "x", 1)
    a = mirrored(z, "x", -1)
    cross = [shift(v, "c", 1) for v in (w, e)]
    q, a, b, cross = lax.optimization_barrier((q, a, b, cross))
    r = mirrored(b, "x", 1)
    last = cross + [shift(v, "c", 1) for v in (z, q, a, b, r)]
    pieces, first = [], 0
    for array in (own, w, e, z, q, a, b, r, core, *last):
        pieces.append((array, first, array.shape[0] // BLK))
        first += array.shape[0] // BLK
    return pieces, ready


PLACE = [[0, 3], [2, 5], [4, 7], [1, 6]]


def fetch(ins, pieces, block, dst, sem, first_row=0, count=BLK):
    for ref, (first, blocks) in zip(ins, pieces):

        @pl.when((block >= first) & (block < first + blocks))
        def _(ref=ref, first=first):
            row = pl.multiple_of((block - first) * BLK + first_row, 64)
            pltpu.make_async_copy(ref.at[pl.ds(row, count), :], dst, sem).start()


def fetched(ins, block, dst, sem, count=BLK):
    @pl.when(block < 0)
    def _():
        dst[...] = jnp.zeros((count, PIV), BF)

    @pl.when(block >= 0)
    def _():
        pltpu.make_async_copy(ins[0].at[pl.ds(0, count), :], dst, sem).wait()


def main_kernel(pieces, dest, chosen, *refs):
    n = len(pieces)
    ins, outs = refs[:n], refs[n : n + 16]
    rows, cols, turned, placed, sem_in, sem_sel, sem_out = refs[n + 16 :]

    for m in range(4):
        fetch(ins, pieces, chosen[m], cols.at[pl.ds(m * BLK, BLK), :], sem_sel.at[m])

    def arrival(i):
        first, blocks = pieces[i]
        return pltpu.make_async_copy(
            ins[i], rows.at[pl.ds(first * BLK, blocks * BLK), :], sem_in.at[i]
        )

    for i in range(n):
        arrival(i).start()

    @pl.loop(0, PORD // 256)
    def _(i):
        for half in range(2):
            placed[half, pl.ds(pl.multiple_of(i * 256, 256), 256), :] = jnp.zeros((256, 256), BF)

    for m in range(4):
        fetched(ins, chosen[m], cols.at[pl.ds(m * BLK, BLK), :], sem_sel.at[m])

    turned[...] = cols[...].T

    def multiply(block, count):
        product = jnp.dot(
            rows[pl.ds(block * BLK, count * BLK), :], turned[...], preferred_element_type=F32
        )
        for b in range(count):
            at = pl.multiple_of(dest[block + b] * BLK, BLK)
            result = (-product[b * BLK : (b + 1) * BLK]).astype(BF)
            placed[0, pl.ds(at, BLK), :] = result[:, :256]
            placed[1, pl.ds(at, BLK), :] = result[:, 256:]

    done, at = 0, 0
    for i in range(n):
        arrival(i).wait()
        done += pieces[i][1]
        if (done - at) % STEP == 0:

            @pl.loop(0, (done - at) // STEP)
            def _(k, at=at):
                multiply(at + k * STEP, STEP)

            at = done

    def leaving(i):
        return pltpu.make_async_copy(
            placed.at[i % 2, pl.ds((i // 2) * 1024, 1024), :], outs[i], sem_out.at[i]
        )

    for i in range(16):
        leaving(i).start()
    for i in range(16):
        leaving(i).wait()


def main_parts(pieces, dest, chosen):
    arrays = [p[0] for p in pieces]
    n = len(arrays)
    outs = pl.pallas_call(
        functools.partial(main_kernel, [p[1:] for p in pieces]),
        out_shape=[jax.ShapeDtypeStruct((1024, 256), BF)] * 16,
        in_specs=[SMEM_SPEC] * 2 + [ANY_SPEC] * n,
        out_specs=[ANY_SPEC] * 16,
        scratch_shapes=[
            pltpu.VMEM((6144, PIV), BF),
            pltpu.VMEM((512, PIV), BF),
            pltpu.VMEM((PIV, 512), BF),
            pltpu.VMEM((2, PORD, 256), BF),
            pltpu.SemaphoreType.DMA((n,)),
            pltpu.SemaphoreType.DMA((4,)),
            pltpu.SemaphoreType.DMA((16,)),
        ],
        compiler_params=pltpu.CompilerParams(vmem_limit_bytes=VMEM_LIMIT),
        cost_estimate=pl.CostEstimate(
            flops=20_000_000_000, bytes_accessed=36_000_000, transcendentals=0
        ),
    )(dest, chosen, *arrays)
    return [[[outs[(dh * 4 + dy) * 2 + k] for k in range(2)] for dy in range(4)] for dh in range(2)]


def panel_kernel(pieces, pan_rows, pan_cols, offset, *refs):
    n = len(pieces)
    ins, out = refs[:n], refs[n]
    left, right, sem_left, sem_right = refs[n + 1 :]
    to_left = lambda q: left.at[pl.ds(q * 64, 64), :]
    to_right = lambda q: right.at[pl.ds(q * BLK, BLK), :]
    for q in range(8):
        fetch(ins, pieces, pan_rows[q], to_left(q), sem_left.at[q], offset[0], 64)
        fetch(ins, pieces, pan_cols[q], to_right(q), sem_right.at[q])
    for q in range(8):
        fetched(ins, pan_rows[q], to_left(q), sem_left.at[q], 64)
    for q in range(8):
        fetched(ins, pan_cols[q], to_right(q), sem_right.at[q])

    for part in range(4):
        product = lax.dot_general(
            left[...],
            right[pl.ds(part * 256, 256), :],
            (((1,), (1,)), ((), ())),
            preferred_element_type=F32,
        )
        out[:, part * 256 : (part + 1) * 256] = (-product).astype(BF)


def panel_parts(pieces, pan_rows, pan_cols, offset):
    arrays = [p[0] for p in pieces]
    n = len(arrays)
    return pl.pallas_call(
        functools.partial(panel_kernel, [p[1:] for p in pieces]),
        out_shape=jax.ShapeDtypeStruct((512, 1024), BF),
        in_specs=[SMEM_SPEC] * 3 + [ANY_SPEC] * n,
        out_specs=pl.BlockSpec(memory_space=pltpu.VMEM),
        scratch_shapes=[
            pltpu.VMEM((512, PIV), BF),
            pltpu.VMEM((1024, PIV), BF),
            pltpu.SemaphoreType.DMA((8,)),
            pltpu.SemaphoreType.DMA((8,)),
        ],
        compiler_params=pltpu.CompilerParams(vmem_limit_bytes=VMEM_LIMIT),
        cost_estimate=pl.CostEstimate(
            flops=2_200_000_000, bytes_accessed=8_000_000, transcendentals=0
        ),
    )(pan_rows, pan_cols, offset, *arrays)


class Ring:
    def __init__(self, term, gate=None):
        carried = term(3).astype(BF)
        if gate is not None:
            carried = after(carried, gate)
        self.marks = []
        for k in (2, 1, 0):
            moved = mirrored(carried, "y", 1)
            self.marks.append(moved)
            self.total = term(k).astype(F32) + moved.astype(F32)
            carried = self.total.astype(BF)


def pick(bit, when_zero, when_one):
    return jnp.where(bit == 0, when_zero, when_one)


def ordered_pair(bit, own, other):
    return jnp.stack([pick(bit, own, other), pick(bit, other, own)])


def ordered_ring(at, parts):
    twice = jnp.stack(list(parts) + list(parts))
    return lax.dynamic_slice_in_dim(twice, (4 - at) % 4, 4, 0)


def front_kernel(pivots, place, front, keep, send, zeros, sems):
    zeros[...] = jnp.zeros_like(zeros)
    for r in range(8):
        columns = pl.ds(r * BLK, BLK)
        local_block = pivots[r] - place[0] * 4
        mine = (local_block >= 0) & (local_block < 4)
        for k, out in enumerate((keep, send)):

            @pl.when(mine)
            def _(k=k, out=out, columns=columns, r=r):
                pltpu.make_async_copy(
                    front.at[:, place[1] ^ k, :, pl.ds(pl.multiple_of(local_block * BLK, BLK), BLK)],
                    out.at[:, :, columns],
                    sems.at[r, k],
                ).start()

            @pl.when(jnp.logical_not(mine))
            def _(k=k, out=out, columns=columns, r=r):
                pltpu.make_async_copy(zeros, out.at[:, :, columns], sems.at[r, k]).start()

    for r in range(8):
        for k, out in enumerate((keep, send)):
            pltpu.make_async_copy(zeros, out.at[:, :, pl.ds(r * BLK, BLK)], sems.at[r, k]).wait()


def front_pick(pivots, place, front):
    return pl.pallas_call(
        front_kernel,
        out_shape=[jax.ShapeDtypeStruct((8, 64, 1024), BF)] * 2,
        in_specs=[SMEM_SPEC] * 2 + [ANY_SPEC],
        out_specs=[ANY_SPEC] * 2,
        scratch_shapes=[pltpu.VMEM((8, 64, BLK), BF), pltpu.SemaphoreType.DMA((8, 2))],
        compiler_params=pltpu.CompilerParams(vmem_limit_bytes=VMEM_LIMIT),
    )(pivots, place, front.reshape(8, 2, 64, 512))


def local(child_panel, child_inverse, child_map, parent_front, parent_inverse, parent_pivots):
    h, y, x, z, c = (lax.axis_index(a) for a in AXES)
    sec = h * 4 + y
    dev = x * 4 + z * 2 + c

    my_map = lax.dynamic_index_in_dim(child_map, sec, 0, keepdims=False)
    place_table = jnp.array(PLACE, jnp.int32)
    child = jnp.arange(48, dtype=jnp.int32)
    owner = child // 3
    place = place_table[
        (owner // 4 - x) * (1 - 2 * (owner % 2)) % 4, (owner // 2 % 2) ^ z
    ]
    position = ((owner % 2) ^ c) * 24 + place * 3 + child % 3
    parent_row = my_map // 8
    slot = (((parent_row // 4) ^ h) * 4 + (parent_row % 4 - y) * (1 - 2 * c) % 4) * 8 + my_map % 8
    dest = jnp.sum(
        jnp.where(position[None, :] == child[:, None], slot[None, :], 0), axis=1, dtype=jnp.int32
    )

    def find(targets):
        hit = my_map[None, :] == targets[:, None]
        return jnp.sum(jnp.where(hit, position[None, :] + 1, 0), axis=1, dtype=jnp.int32) - 1

    chosen = find(dev * 4 + jnp.arange(4, dtype=jnp.int32))
    pan_rows = find(jnp.arange(8, dtype=jnp.int32) * 8 + dev // 2)
    pan_cols = find(parent_pivots)
    offset = (dev % 2 * 64).astype(jnp.int32).reshape(1)

    keep, send = front_pick(parent_pivots, jnp.stack([dev, c]).astype(jnp.int32), parent_front)
    front = (keep + shift(send, "c", 1)).reshape(4, 2, 64, 1024)
    front_x = [lax.dynamic_index_in_dim(front, (x + k) % 4, 0, keepdims=False) for k in range(4)]

    pieces, ready = gather_rows(
        factor(child_panel, child_inverse), (dest, chosen, pan_rows, pan_cols, offset, front_x)
    )
    dest, chosen, pan_rows, pan_cols, offset, front_x = ready

    pan = panel_parts(pieces, pan_rows, pan_cols, offset)
    arrived = lax.all_to_all(
        pan.reshape(8, 64, 1024), ("h", "y"), split_axis=0, concat_axis=0, tiled=True
    )
    main = main_parts(pieces, dest, chosen)

    front_x = [after(v, pan) for v in front_x]
    front_z = (
        front_x[0]
        + shift(front_x[1], "x", 1)
        + shift(front_x[3], "x", -1)
        + shift(front_x[2], "x", 2)
    )
    front_rows = pick(z, front_z[0], front_z[1]) + shift(pick(z, front_z[1], front_z[0]), "z", 1)

    arrived, main = lax.optimization_barrier((arrived, main))
    pan_rows_f = arrived.astype(F32).sum(axis=0) + front_rows.astype(F32)
    share = jnp.dot(pan_rows_f.astype(BF), parent_inverse, preferred_element_type=F32).astype(BF)

    rings = []
    for d in (1, 0):
        for half in range(2):
            rings.append(
                Ring(
                    lambda k: main[d][k][half],
                    None if d == 1 else rings[half].marks[0],
                )
            )
    far = [shift(ring.total.astype(BF), "h", 1).astype(F32) for ring in rings[:2]]
    near = jnp.concatenate([rings[2].total + far[0], rings[3].total + far[1]], axis=1)
    assembled = parent_front.astype(F32) + near

    row_block = sec * 8 + dev // 2
    masked = jnp.where(jnp.any(parent_pivots == row_block), jnp.zeros_like(share), share)
    masked = after(masked, rings[0].marks[0])
    pairs = [(s * 16 + d, (d % 8) * 16 + 2 * s + d // 8) for s in range(8) for d in range(16)]
    moved = lax.ppermute(masked, AXES, pairs)
    both = ordered_pair(h, moved, shift(moved, "h", 1))
    share = after(share, both)
    both = after(both, rings[1].marks[1])
    ring = ordered_ring(y, [both, shift(both, "y", -1), shift(both, "y", 2), shift(both, "y", 1)])
    column_factor = ring.transpose(1, 0, 2, 3).reshape(512, 1024)

    copies = jnp.broadcast_to(share, (16, 64, 1024))
    parent_factor = lax.all_to_all(
        copies, ("x", "z", "c"), split_axis=0, concat_axis=0, tiled=True
    ).reshape(1024, 1024)

    my_blocks = sec * 8 + jnp.arange(8, dtype=jnp.int32)
    is_pivot = jnp.any(parent_pivots[None, :] == my_blocks[:, None], axis=1)
    row_pivot = jnp.repeat(is_pivot, BLK)
    trailing = jnp.where(row_pivot[:, None], jnp.zeros_like(parent_factor), parent_factor)
    update = lax.dot_general(
        trailing, column_factor, (((1,), (1,)), ((), ())), preferred_element_type=F32
    )
    update = lax.optimization_barrier(update)
    parent_factor = jnp.where(parent_pivots[0] < 0, jnp.zeros_like(parent_factor), parent_factor)
    return assembled - update, parent_factor


def solution(mesh):
    fine = Mesh(mesh.devices.reshape(tuple(SIZE[a] for a in AXES)), AXES)
    sec, dev = ("h", "y"), ("x", "z", "c")
    placed = (P(sec, dev, None), P(sec, None, None), P(), P(sec, dev), P(), P())
    return jax.shard_map(
        local,
        mesh=fine,
        in_specs=placed,
        out_specs=(P(sec, dev), P(sec, None)),
        check_vma=False,
    )
```

```python
import functools

import jax
import jax.numpy as jnp
from jax import lax
from jax.experimental import pallas as pl
from jax.experimental.pallas import tpu as pltpu
from jax.sharding import Mesh
from jax.sharding import PartitionSpec as P

BLK = 128
PORD = 8192
PIV = 2048
KH = PIV // 2
OWN = 384
STEP = 12
BF = jnp.bfloat16
F32 = jnp.float32
VMEM_LIMIT = 60 * 2**20
SMEM_SPEC = pl.BlockSpec(memory_space=pltpu.SMEM)
ANY_SPEC = pl.BlockSpec(memory_space=pl.ANY)
SIZE = {"h": 2, "y": 4, "x": 4, "z": 2, "c": 2}
AXES = ("h", "y", "x", "z", "c")
def shift(array, axis, step):
    size = SIZE[axis]
    return lax.ppermute(array, axis, [(i, (i + step) % size) for i in range(size)])


def mirrored(array, axis, step):
    size = SIZE[axis]
    pairs = [
        (i * 2 + core, (i + (step if core == 0 else -step)) % size * 2 + core)
        for i in range(size)
        for core in range(2)
    ]
    return lax.ppermute(array, (axis, "c"), pairs)


def after(value, *earlier):
    return lax.optimization_barrier((value,) + earlier)[0]


def factor_kernel(panel, inverse, out, held, sems):
    width = 512
    for j in range(PIV // width):
        deep = (j + 1) * width
        pltpu.make_async_copy(
            inverse.at[0, pl.ds(0, deep), pl.ds(j * width, width)],
            held.at[pl.ds(0, deep), pl.ds(j * width, width)],
            sems.at[j],
        ).start()
    for j in range(PIV // width):
        deep = (j + 1) * width
        pltpu.make_async_copy(
            inverse.at[0, pl.ds(0, deep), pl.ds(j * width, width)],
            held.at[pl.ds(0, deep), pl.ds(j * width, width)],
            sems.at[j],
        ).wait()
        out[:, j * width : deep] = jnp.dot(
            panel[0, :, :deep], held[:deep, j * width : deep], preferred_element_type=F32
        ).astype(BF)


def factor(panel, inverse):
    vmem = pl.BlockSpec(memory_space=pltpu.VMEM)
    return pl.pallas_call(
        factor_kernel,
        out_shape=jax.ShapeDtypeStruct((OWN, PIV), BF),
        in_specs=[vmem, ANY_SPEC],
        out_specs=vmem,
        scratch_shapes=[pltpu.VMEM((PIV, PIV), BF), pltpu.SemaphoreType.DMA((4,))],
        compiler_params=pltpu.CompilerParams(vmem_limit_bytes=VMEM_LIMIT),
        cost_estimate=pl.CostEstimate(
            flops=2_000_000_000, bytes_accessed=8_000_000, transcendentals=0
        ),
    )(panel, inverse)


def gather_rows(own, ready):
    w = mirrored(own, "x", 1)
    e = mirrored(own, "x", -1)
    z = shift(own, "z", 1)
    core = shift(own, "c", 1)
    w, e, z, core, ready = lax.optimization_barrier((w, e, z, core, ready))
    b = shift(w, "z", 1)
    q = mirrored(w, "x", 1)
    a = mirrored(z, "x", -1)
    cross = [shift(v, "c", 1) for v in (w, e)]
    q, a, b, cross = lax.optimization_barrier((q, a, b, cross))
    r = mirrored(b, "x", 1)
    last = cross + [shift(v, "c", 1) for v in (z, q, a, b, r)]
    pieces, first = [], 0
    for array in (own, w, e, z, q, a, b, r, core, *last):
        pieces.append((array, first, array.shape[0] // BLK))
        first += array.shape[0] // BLK
    return pieces, ready


PLACE = [[0, 3], [2, 5], [4, 7], [1, 6]]


def fetch(ins, pieces, block, dst, sem, first_row=0, count=BLK):
    for ref, (first, blocks) in zip(ins, pieces):

        @pl.when((block >= first) & (block < first + blocks))
        def _(ref=ref, first=first):
            row = pl.multiple_of((block - first) * BLK + first_row, 64)
            pltpu.make_async_copy(ref.at[pl.ds(row, count), :], dst, sem).start()


def fetched(ins, block, dst, sem, count=BLK):
    @pl.when(block < 0)
    def _():
        dst[...] = jnp.zeros((count, PIV), BF)

    @pl.when(block >= 0)
    def _():
        pltpu.make_async_copy(ins[0].at[pl.ds(0, count), :], dst, sem).wait()


def main_kernel(pieces, dest, chosen, *refs):
    n = len(pieces)
    ins, outs = refs[:n], refs[n : n + 16]
    rows, cols, turned, placed, sem_in, sem_sel, sem_out = refs[n + 16 :]

    for m in range(4):
        fetch(ins, pieces, chosen[m], cols.at[pl.ds(m * BLK, BLK), :], sem_sel.at[m])

    def arrival(i):
        first, blocks = pieces[i]
        return pltpu.make_async_copy(
            ins[i], rows.at[pl.ds(first * BLK, blocks * BLK), :], sem_in.at[i]
        )

    early = 4
    for i in range(early):
        arrival(i).start()

    @pl.loop(0, PORD // 256)
    def _(i):
        for half in range(2):
            placed[half, pl.ds(pl.multiple_of(i * 256, 256), 256), :] = jnp.zeros((256, 256), BF)

    for m in range(4):
        fetched(ins, chosen[m], cols.at[pl.ds(m * BLK, BLK), :], sem_sel.at[m])
    for i in range(early, n):
        arrival(i).start()

    turned[...] = cols[...].T

    def multiply(block, count):
        product = jnp.dot(
            rows[pl.ds(block * BLK, count * BLK), :], turned[...], preferred_element_type=F32
        )
        for b in range(count):
            at = pl.multiple_of(dest[block + b] * BLK, BLK)
            result = (-product[b * BLK : (b + 1) * BLK]).astype(BF)
            placed[0, pl.ds(at, BLK), :] = result[:, :256]
            placed[1, pl.ds(at, BLK), :] = result[:, 256:]

    done, at = 0, 0
    for i in range(n):
        arrival(i).wait()
        done += pieces[i][1]
        if (done - at) % STEP == 0:

            @pl.loop(0, (done - at) // STEP)
            def _(k, at=at):
                multiply(at + k * STEP, STEP)

            at = done

    def leaving(i):
        return pltpu.make_async_copy(
            placed.at[i % 2, pl.ds((i // 2) * 1024, 1024), :], outs[i], sem_out.at[i]
        )

    for i in range(16):
        leaving(i).start()
    for i in range(16):
        leaving(i).wait()


def main_parts(pieces, dest, chosen):
    arrays = [p[0] for p in pieces]
    n = len(arrays)
    outs = pl.pallas_call(
        functools.partial(main_kernel, [p[1:] for p in pieces]),
        out_shape=[jax.ShapeDtypeStruct((1024, 256), BF)] * 16,
        in_specs=[SMEM_SPEC] * 2 + [ANY_SPEC] * n,
        out_specs=[ANY_SPEC] * 16,
        scratch_shapes=[
            pltpu.VMEM((6144, PIV), BF),
            pltpu.VMEM((512, PIV), BF),
            pltpu.VMEM((PIV, 512), BF),
            pltpu.VMEM((2, PORD, 256), BF),
            pltpu.SemaphoreType.DMA((n,)),
            pltpu.SemaphoreType.DMA((4,)),
            pltpu.SemaphoreType.DMA((16,)),
        ],
        compiler_params=pltpu.CompilerParams(vmem_limit_bytes=VMEM_LIMIT),
        cost_estimate=pl.CostEstimate(
            flops=20_000_000_000, bytes_accessed=36_000_000, transcendentals=0
        ),
    )(dest, chosen, *arrays)
    return [[[outs[(dh * 4 + dy) * 2 + k] for k in range(2)] for dy in range(4)] for dh in range(2)]


def panel_kernel(pieces, pan_rows, pan_cols, offset, *refs):
    n = len(pieces)
    ins, out = refs[:n], refs[n]
    left, right, sem_left, sem_right = refs[n + 1 :]
    to_left = lambda q: left.at[pl.ds(q * 64, 64), :]
    to_right = lambda q: right.at[pl.ds(q * BLK, BLK), :]
    for q in range(8):
        fetch(ins, pieces, pan_rows[q], to_left(q), sem_left.at[q], offset[0], 64)
        fetch(ins, pieces, pan_cols[q], to_right(q), sem_right.at[q])
    for q in range(8):
        fetched(ins, pan_rows[q], to_left(q), sem_left.at[q], 64)
    for q in range(8):
        fetched(ins, pan_cols[q], to_right(q), sem_right.at[q])

    for part in range(4):
        product = lax.dot_general(
            left[...],
            right[pl.ds(part * 256, 256), :],
            (((1,), (1,)), ((), ())),
            preferred_element_type=F32,
        )
        out[:, part * 256 : (part + 1) * 256] = (-product).astype(BF)


def panel_parts(pieces, pan_rows, pan_cols, offset):
    arrays = [p[0] for p in pieces]
    n = len(arrays)
    return pl.pallas_call(
        functools.partial(panel_kernel, [p[1:] for p in pieces]),
        out_shape=jax.ShapeDtypeStruct((512, 1024), BF),
        in_specs=[SMEM_SPEC] * 3 + [ANY_SPEC] * n,
        out_specs=pl.BlockSpec(memory_space=pltpu.VMEM),
        scratch_shapes=[
            pltpu.VMEM((512, PIV), BF),
            pltpu.VMEM((1024, PIV), BF),
            pltpu.SemaphoreType.DMA((8,)),
            pltpu.SemaphoreType.DMA((8,)),
        ],
        compiler_params=pltpu.CompilerParams(vmem_limit_bytes=VMEM_LIMIT),
        cost_estimate=pl.CostEstimate(
            flops=2_200_000_000, bytes_accessed=8_000_000, transcendentals=0
        ),
    )(pan_rows, pan_cols, offset, *arrays)


class Ring:
    def __init__(self, term, gate=None):
        carried = term(3).astype(BF)
        if gate is not None:
            carried = after(carried, gate)
        self.marks = []
        for k in (2, 1, 0):
            moved = mirrored(carried, "y", 1)
            self.marks.append(moved)
            self.total = term(k).astype(F32) + moved.astype(F32)
            carried = self.total.astype(BF)


def pick(bit, when_zero, when_one):
    return jnp.where(bit == 0, when_zero, when_one)


def ordered_pair(bit, own, other):
    return jnp.stack([pick(bit, own, other), pick(bit, other, own)])


def ordered_ring(at, parts):
    twice = jnp.stack(list(parts) + list(parts))
    return lax.dynamic_slice_in_dim(twice, (4 - at) % 4, 4, 0)


def front_kernel(pivots, place, front, keep, send, zeros, sems):
    zeros[...] = jnp.zeros_like(zeros)
    for r in range(8):
        columns = pl.ds(r * BLK, BLK)
        local_block = pivots[r] - place[0] * 4
        mine = (local_block >= 0) & (local_block < 4)
        for k, out in enumerate((keep, send)):

            @pl.when(mine)
            def _(k=k, out=out, columns=columns, r=r):
                pltpu.make_async_copy(
                    front.at[:, place[1] ^ k, :, pl.ds(pl.multiple_of(local_block * BLK, BLK), BLK)],
                    out.at[:, :, columns],
                    sems.at[r, k],
                ).start()

            @pl.when(jnp.logical_not(mine))
            def _(k=k, out=out, columns=columns, r=r):
                pltpu.make_async_copy(zeros, out.at[:, :, columns], sems.at[r, k]).start()

    for r in range(8):
        for k, out in enumerate((keep, send)):
            pltpu.make_async_copy(zeros, out.at[:, :, pl.ds(r * BLK, BLK)], sems.at[r, k]).wait()


def front_pick(pivots, place, front):
    return pl.pallas_call(
        front_kernel,
        out_shape=[jax.ShapeDtypeStruct((8, 64, 1024), BF)] * 2,
        in_specs=[SMEM_SPEC] * 2 + [ANY_SPEC],
        out_specs=[ANY_SPEC] * 2,
        scratch_shapes=[pltpu.VMEM((8, 64, BLK), BF), pltpu.SemaphoreType.DMA((8, 2))],
        compiler_params=pltpu.CompilerParams(vmem_limit_bytes=VMEM_LIMIT),
    )(pivots, place, front.reshape(8, 2, 64, 512))


def local(child_panel, child_inverse, child_map, parent_front, parent_inverse, parent_pivots):
    h, y, x, z, c = (lax.axis_index(a) for a in AXES)
    sec = h * 4 + y
    dev = x * 4 + z * 2 + c

    my_map = lax.dynamic_index_in_dim(child_map, sec, 0, keepdims=False)
    place_table = jnp.array(PLACE, jnp.int32)
    child = jnp.arange(48, dtype=jnp.int32)
    owner = child // 3
    place = place_table[
        (owner // 4 - x) * (1 - 2 * (owner % 2)) % 4, (owner // 2 % 2) ^ z
    ]
    position = ((owner % 2) ^ c) * 24 + place * 3 + child % 3
    parent_row = my_map // 8
    slot = (((parent_row // 4) ^ h) * 4 + (parent_row % 4 - y) * (1 - 2 * c) % 4) * 8 + my_map % 8
    dest = jnp.sum(
        jnp.where(position[None, :] == child[:, None], slot[None, :], 0), axis=1, dtype=jnp.int32
    )

    def find(targets):
        hit = my_map[None, :] == targets[:, None]
        return jnp.sum(jnp.where(hit, position[None, :] + 1, 0), axis=1, dtype=jnp.int32) - 1

    chosen = find(dev * 4 + jnp.arange(4, dtype=jnp.int32))
    pan_rows = find(jnp.arange(8, dtype=jnp.int32) * 8 + dev // 2)
    pan_cols = find(parent_pivots)
    offset = (dev % 2 * 64).astype(jnp.int32).reshape(1)

    keep, send = front_pick(parent_pivots, jnp.stack([dev, c]).astype(jnp.int32), parent_front)
    front = (keep + shift(send, "c", 1)).reshape(4, 2, 64, 1024)
    front_x = [lax.dynamic_index_in_dim(front, (x + k) % 4, 0, keepdims=False) for k in range(4)]

    pieces, ready = gather_rows(
        factor(child_panel, child_inverse), (dest, chosen, pan_rows, pan_cols, offset, front_x)
    )
    dest, chosen, pan_rows, pan_cols, offset, front_x = ready

    pan = panel_parts(pieces, pan_rows, pan_cols, offset)
    arrived = lax.all_to_all(
        pan.reshape(8, 64, 1024), ("h", "y"), split_axis=0, concat_axis=0, tiled=True
    )
    main = main_parts(pieces, dest, chosen)

    front_x = [after(v, pan) for v in front_x]
    front_z = (
        front_x[0]
        + shift(front_x[1], "x", 1)
        + shift(front_x[3], "x", -1)
        + shift(front_x[2], "x", 2)
    )
    front_rows = pick(z, front_z[0], front_z[1]) + shift(pick(z, front_z[1], front_z[0]), "z", 1)

    arrived, main = lax.optimization_barrier((arrived, main))
    pan_rows_f = arrived.astype(F32).sum(axis=0) + front_rows.astype(F32)
    share = jnp.dot(pan_rows_f.astype(BF), parent_inverse, preferred_element_type=F32).astype(BF)

    rings = []
    for d in (1, 0):
        for half in range(2):
            rings.append(
                Ring(
                    lambda k: main[d][k][half],
                    None if d == 1 or half == 0 else rings[half].marks[0],
                )
            )
    far = [shift(ring.total.astype(BF), "h", 1).astype(F32) for ring in rings[:2]]
    near = jnp.concatenate([rings[2].total + far[0], rings[3].total + far[1]], axis=1)
    assembled = parent_front.astype(F32) + near

    row_block = sec * 8 + dev // 2
    masked = jnp.where(jnp.any(parent_pivots == row_block), jnp.zeros_like(share), share)
    masked = after(masked, rings[0].marks[0])
    pairs = [(s * 16 + d, (d % 8) * 16 + 2 * s + d // 8) for s in range(8) for d in range(16)]
    moved = lax.ppermute(masked, AXES, pairs)
    both = ordered_pair(h, moved, shift(moved, "h", 1))
    share = after(share, both)
    both = after(both, rings[1].marks[1])
    ring = ordered_ring(y, [both, shift(both, "y", -1), shift(both, "y", 2), shift(both, "y", 1)])
    column_factor = ring.transpose(1, 0, 2, 3).reshape(512, 1024)

    copies = jnp.broadcast_to(share, (16, 64, 1024))
    parent_factor = lax.all_to_all(
        copies, ("x", "z", "c"), split_axis=0, concat_axis=0, tiled=True
    ).reshape(1024, 1024)

    my_blocks = sec * 8 + jnp.arange(8, dtype=jnp.int32)
    is_pivot = jnp.any(parent_pivots[None, :] == my_blocks[:, None], axis=1)
    row_pivot = jnp.repeat(is_pivot, BLK)
    trailing = jnp.where(row_pivot[:, None], jnp.zeros_like(parent_factor), parent_factor)
    update = lax.dot_general(
        trailing, column_factor, (((1,), (1,)), ((), ())), preferred_element_type=F32
    )
    update = lax.optimization_barrier(update)
    parent_factor = jnp.where(parent_pivots[0] < 0, jnp.zeros_like(parent_factor), parent_factor)
    return assembled - update, parent_factor


def solution(mesh):
    fine = Mesh(mesh.devices.reshape(tuple(SIZE[a] for a in AXES)), AXES)
    sec, dev = ("h", "y"), ("x", "z", "c")
    placed = (P(sec, dev, None), P(sec, None, None), P(), P(sec, dev), P(), P())
    return jax.shard_map(
        local,
        mesh=fine,
        in_specs=placed,
        out_specs=(P(sec, dev), P(sec, None)),
        check_vma=False,
    )
```

```python
import functools

import jax
import jax.numpy as jnp
from jax import lax
from jax.experimental import pallas as pl
from jax.experimental.pallas import tpu as pltpu
from jax.sharding import Mesh
from jax.sharding import PartitionSpec as P

BLK = 128
PORD = 8192
PIV = 2048
KH = PIV // 2
OWN = 384
STEP = 12
BF = jnp.bfloat16
F32 = jnp.float32
VMEM_LIMIT = 60 * 2**20
SMEM_SPEC = pl.BlockSpec(memory_space=pltpu.SMEM)
ANY_SPEC = pl.BlockSpec(memory_space=pl.ANY)
SIZE = {"h": 2, "y": 4, "x": 4, "z": 2, "c": 2}
AXES = ("h", "y", "x", "z", "c")
def shift(array, axis, step):
    size = SIZE[axis]
    return lax.ppermute(array, axis, [(i, (i + step) % size) for i in range(size)])


def mirrored(array, axis, step):
    size = SIZE[axis]
    pairs = [
        (i * 2 + core, (i + (step if core == 0 else -step)) % size * 2 + core)
        for i in range(size)
        for core in range(2)
    ]
    return lax.ppermute(array, (axis, "c"), pairs)


def after(value, *earlier):
    return lax.optimization_barrier((value,) + earlier)[0]


def factor_kernel(panel, inverse, out, held, sems):
    width = 512
    for j in range(PIV // width):
        deep = (j + 1) * width
        pltpu.make_async_copy(
            inverse.at[0, pl.ds(0, deep), pl.ds(j * width, width)],
            held.at[pl.ds(0, deep), pl.ds(j * width, width)],
            sems.at[j],
        ).start()
    for j in range(PIV // width):
        deep = (j + 1) * width
        pltpu.make_async_copy(
            inverse.at[0, pl.ds(0, deep), pl.ds(j * width, width)],
            held.at[pl.ds(0, deep), pl.ds(j * width, width)],
            sems.at[j],
        ).wait()
        out[:, j * width : deep] = jnp.dot(
            panel[0, :, :deep], held[:deep, j * width : deep], preferred_element_type=F32
        ).astype(BF)


def factor(panel, inverse):
    vmem = pl.BlockSpec(memory_space=pltpu.VMEM)
    return pl.pallas_call(
        factor_kernel,
        out_shape=jax.ShapeDtypeStruct((OWN, PIV), BF),
        in_specs=[vmem, ANY_SPEC],
        out_specs=vmem,
        scratch_shapes=[pltpu.VMEM((PIV, PIV), BF), pltpu.SemaphoreType.DMA((4,))],
        compiler_params=pltpu.CompilerParams(vmem_limit_bytes=VMEM_LIMIT),
        cost_estimate=pl.CostEstimate(
            flops=2_000_000_000, bytes_accessed=8_000_000, transcendentals=0
        ),
    )(panel, inverse)


def gather_rows(own, ready):
    w = mirrored(own, "x", 1)
    e = mirrored(own, "x", -1)
    z = shift(own, "z", 1)
    core = shift(own, "c", 1)
    w, e, z, core, ready = lax.optimization_barrier((w, e, z, core, ready))
    b = shift(w, "z", 1)
    q = mirrored(w, "x", 1)
    a = mirrored(z, "x", -1)
    cross = [shift(v, "c", 1) for v in (w, e)]
    q, a, b, cross = lax.optimization_barrier((q, a, b, cross))
    r = mirrored(b, "x", 1)
    last = cross + [shift(v, "c", 1) for v in (z, q, a, b, r)]
    pieces, first = [], 0
    for array in (own, w, e, z, q, a, b, r, core, *last):
        pieces.append((array, first, array.shape[0] // BLK))
        first += array.shape[0] // BLK
    return pieces, ready


PLACE = [[0, 3], [2, 5], [4, 7], [1, 6]]


def fetch(ins, pieces, block, dst, sem, first_row=0, count=BLK):
    for ref, (first, blocks) in zip(ins, pieces):

        @pl.when((block >= first) & (block < first + blocks))
        def _(ref=ref, first=first):
            row = pl.multiple_of((block - first) * BLK + first_row, 64)
            pltpu.make_async_copy(ref.at[pl.ds(row, count), :], dst, sem).start()


def fetched(ins, block, dst, sem, count=BLK):
    @pl.when(block < 0)
    def _():
        dst[...] = jnp.zeros((count, PIV), BF)

    @pl.when(block >= 0)
    def _():
        pltpu.make_async_copy(ins[0].at[pl.ds(0, count), :], dst, sem).wait()


def main_kernel(pieces, dest, chosen, *refs):
    n = len(pieces)
    ins, outs = refs[:n], refs[n : n + 16]
    rows, cols, turned, placed, sem_in, sem_sel, sem_out = refs[n + 16 :]

    for m in range(4):
        fetch(ins, pieces, chosen[m], cols.at[pl.ds(m * BLK, BLK), :], sem_sel.at[m])

    def arrival(i):
        first, blocks = pieces[i]
        return pltpu.make_async_copy(
            ins[i], rows.at[pl.ds(first * BLK, blocks * BLK), :], sem_in.at[i]
        )

    early = 4
    for i in range(early):
        arrival(i).start()

    @pl.loop(0, PORD // 256)
    def _(i):
        for half in range(2):
            placed[half, pl.ds(pl.multiple_of(i * 256, 256), 256), :] = jnp.zeros((256, 256), BF)

    for m in range(4):
        fetched(ins, chosen[m], cols.at[pl.ds(m * BLK, BLK), :], sem_sel.at[m])
    for i in range(early, n):
        arrival(i).start()

    turned[...] = cols[...].T

    def multiply(block, count):
        product = jnp.dot(
            rows[pl.ds(block * BLK, count * BLK), :], turned[...], preferred_element_type=F32
        )
        for b in range(count):
            at = pl.multiple_of(dest[block + b] * BLK, BLK)
            result = (-product[b * BLK : (b + 1) * BLK]).astype(BF)
            placed[0, pl.ds(at, BLK), :] = result[:, :256]
            placed[1, pl.ds(at, BLK), :] = result[:, 256:]

    done, at = 0, 0
    for i in range(n):
        arrival(i).wait()
        done += pieces[i][1]
        if (done - at) % STEP == 0:

            @pl.loop(0, (done - at) // STEP)
            def _(k, at=at):
                multiply(at + k * STEP, STEP)

            at = done

    def leaving(i):
        return pltpu.make_async_copy(
            placed.at[i % 2, pl.ds((i // 2) * 1024, 1024), :], outs[i], sem_out.at[i]
        )

    for i in range(16):
        leaving(i).start()
    for i in range(16):
        leaving(i).wait()


def main_parts(pieces, dest, chosen):
    arrays = [p[0] for p in pieces]
    n = len(arrays)
    outs = pl.pallas_call(
        functools.partial(main_kernel, [p[1:] for p in pieces]),
        out_shape=[jax.ShapeDtypeStruct((1024, 256), BF)] * 16,
        in_specs=[SMEM_SPEC] * 2 + [ANY_SPEC] * n,
        out_specs=[ANY_SPEC] * 16,
        scratch_shapes=[
            pltpu.VMEM((6144, PIV), BF),
            pltpu.VMEM((512, PIV), BF),
            pltpu.VMEM((PIV, 512), BF),
            pltpu.VMEM((2, PORD, 256), BF),
            pltpu.SemaphoreType.DMA((n,)),
            pltpu.SemaphoreType.DMA((4,)),
            pltpu.SemaphoreType.DMA((16,)),
        ],
        compiler_params=pltpu.CompilerParams(vmem_limit_bytes=VMEM_LIMIT),
        cost_estimate=pl.CostEstimate(
            flops=20_000_000_000, bytes_accessed=36_000_000, transcendentals=0
        ),
    )(dest, chosen, *arrays)
    return [[[outs[(dh * 4 + dy) * 2 + k] for k in range(2)] for dy in range(4)] for dh in range(2)]


def panel_kernel(pieces, pan_rows, pan_cols, offset, *refs):
    n = len(pieces)
    ins, out = refs[:n], refs[n]
    left, right, sem_left, sem_right = refs[n + 1 :]
    to_left = lambda q: left.at[pl.ds(q * 64, 64), :]
    to_right = lambda q: right.at[pl.ds(q * BLK, BLK), :]
    for q in range(8):
        fetch(ins, pieces, pan_rows[q], to_left(q), sem_left.at[q], offset[0], 64)
        fetch(ins, pieces, pan_cols[q], to_right(q), sem_right.at[q])
    for q in range(8):
        fetched(ins, pan_rows[q], to_left(q), sem_left.at[q], 64)
    for q in range(8):
        fetched(ins, pan_cols[q], to_right(q), sem_right.at[q])

    for part in range(4):
        product = lax.dot_general(
            left[...],
            right[pl.ds(part * 256, 256), :],
            (((1,), (1,)), ((), ())),
            preferred_element_type=F32,
        )
        out[:, part * 256 : (part + 1) * 256] = (-product).astype(BF)


def panel_parts(pieces, pan_rows, pan_cols, offset):
    arrays = [p[0] for p in pieces]
    n = len(arrays)
    return pl.pallas_call(
        functools.partial(panel_kernel, [p[1:] for p in pieces]),
        out_shape=jax.ShapeDtypeStruct((512, 1024), BF),
        in_specs=[SMEM_SPEC] * 3 + [ANY_SPEC] * n,
        out_specs=pl.BlockSpec(memory_space=pltpu.VMEM),
        scratch_shapes=[
            pltpu.VMEM((512, PIV), BF),
            pltpu.VMEM((1024, PIV), BF),
            pltpu.SemaphoreType.DMA((8,)),
            pltpu.SemaphoreType.DMA((8,)),
        ],
        compiler_params=pltpu.CompilerParams(vmem_limit_bytes=VMEM_LIMIT),
        cost_estimate=pl.CostEstimate(
            flops=2_200_000_000, bytes_accessed=8_000_000, transcendentals=0
        ),
    )(pan_rows, pan_cols, offset, *arrays)


class Ring:
    def __init__(self, term, gate=None):
        carried = term(3).astype(BF)
        if gate is not None:
            carried = after(carried, gate)
        self.marks = []
        for k in (2, 1, 0):
            moved = mirrored(carried, "y", 1)
            self.marks.append(moved)
            self.total = term(k).astype(F32) + moved.astype(F32)
            carried = self.total.astype(BF)


def pick(bit, when_zero, when_one):
    return jnp.where(bit == 0, when_zero, when_one)


def ordered_pair(bit, own, other):
    return jnp.stack([pick(bit, own, other), pick(bit, other, own)])


def ordered_ring(at, parts):
    twice = jnp.stack(list(parts) + list(parts))
    return lax.dynamic_slice_in_dim(twice, (4 - at) % 4, 4, 0)


def front_kernel(pivots, place, front, keep, send, zeros, sems):
    zeros[...] = jnp.zeros_like(zeros)
    for r in range(8):
        columns = pl.ds(r * BLK, BLK)
        local_block = pivots[r] - place[0] * 4
        mine = (local_block >= 0) & (local_block < 4)
        for k, out in enumerate((keep, send)):

            @pl.when(mine)
            def _(k=k, out=out, columns=columns, r=r):
                pltpu.make_async_copy(
                    front.at[:, place[1] ^ k, :, pl.ds(pl.multiple_of(local_block * BLK, BLK), BLK)],
                    out.at[:, :, columns],
                    sems.at[r, k],
                ).start()

            @pl.when(jnp.logical_not(mine))
            def _(k=k, out=out, columns=columns, r=r):
                pltpu.make_async_copy(zeros, out.at[:, :, columns], sems.at[r, k]).start()

    for r in range(8):
        for k, out in enumerate((keep, send)):
            pltpu.make_async_copy(zeros, out.at[:, :, pl.ds(r * BLK, BLK)], sems.at[r, k]).wait()


def front_pick(pivots, place, front):
    return pl.pallas_call(
        front_kernel,
        out_shape=[jax.ShapeDtypeStruct((8, 64, 1024), BF)] * 2,
        in_specs=[SMEM_SPEC] * 2 + [ANY_SPEC],
        out_specs=[ANY_SPEC] * 2,
        scratch_shapes=[pltpu.VMEM((8, 64, BLK), BF), pltpu.SemaphoreType.DMA((8, 2))],
        compiler_params=pltpu.CompilerParams(vmem_limit_bytes=VMEM_LIMIT),
    )(pivots, place, front.reshape(8, 2, 64, 512))


def local(child_panel, child_inverse, child_map, parent_front, parent_inverse, parent_pivots):
    h, y, x, z, c = (lax.axis_index(a) for a in AXES)
    sec = h * 4 + y
    dev = x * 4 + z * 2 + c

    my_map = lax.dynamic_index_in_dim(child_map, sec, 0, keepdims=False)
    place_table = jnp.array(PLACE, jnp.int32)
    child = jnp.arange(48, dtype=jnp.int32)
    owner = child // 3
    place = place_table[
        (owner // 4 - x) * (1 - 2 * (owner % 2)) % 4, (owner // 2 % 2) ^ z
    ]
    position = ((owner % 2) ^ c) * 24 + place * 3 + child % 3
    parent_row = my_map // 8
    slot = (((parent_row // 4) ^ h) * 4 + (parent_row % 4 - y) * (1 - 2 * c) % 4) * 8 + my_map % 8
    dest = jnp.sum(
        jnp.where(position[None, :] == child[:, None], slot[None, :], 0), axis=1, dtype=jnp.int32
    )

    def find(targets):
        hit = my_map[None, :] == targets[:, None]
        return jnp.sum(jnp.where(hit, position[None, :] + 1, 0), axis=1, dtype=jnp.int32) - 1

    chosen = find(dev * 4 + jnp.arange(4, dtype=jnp.int32))
    pan_rows = find(jnp.arange(8, dtype=jnp.int32) * 8 + dev // 2)
    pan_cols = find(parent_pivots)
    offset = (dev % 2 * 64).astype(jnp.int32).reshape(1)

    keep, send = front_pick(parent_pivots, jnp.stack([dev, c]).astype(jnp.int32), parent_front)
    front = (keep + shift(send, "c", 1)).reshape(4, 2, 64, 1024)
    front_x = [lax.dynamic_index_in_dim(front, (x + k) % 4, 0, keepdims=False) for k in range(4)]

    pieces, ready = gather_rows(
        factor(child_panel, child_inverse), (dest, chosen, pan_rows, pan_cols, offset, front_x)
    )
    dest, chosen, pan_rows, pan_cols, offset, front_x = ready

    pan = panel_parts(pieces, pan_rows, pan_cols, offset)
    arrived = lax.all_to_all(
        pan.reshape(8, 64, 1024), ("h", "y"), split_axis=0, concat_axis=0, tiled=True
    )
    main = main_parts(pieces, dest, chosen)

    front_x = [after(v, pan) for v in front_x]
    front_z = (
        front_x[0]
        + shift(front_x[1], "x", 1)
        + shift(front_x[3], "x", -1)
        + shift(front_x[2], "x", 2)
    )
    front_rows = pick(z, front_z[0], front_z[1]) + shift(pick(z, front_z[1], front_z[0]), "z", 1)

    arrived, main = lax.optimization_barrier((arrived, main))
    pan_rows_f = arrived.astype(F32).sum(axis=0) + front_rows.astype(F32)
    share = jnp.dot(pan_rows_f.astype(BF), parent_inverse, preferred_element_type=F32).astype(BF)

    rings = []
    for d in (1, 0):
        for half in range(2):
            rings.append(
                Ring(
                    lambda k: main[d][k][half],
                    None if d == 1 else rings[half].marks[0],
                )
            )
    swapped = [shift(ring.total.astype(BF), "h", 1) for ring in rings[:2]]
    far = [v.astype(F32) for v in swapped]
    near = jnp.concatenate([rings[2].total + far[0], rings[3].total + far[1]], axis=1)
    assembled = parent_front.astype(F32) + near

    row_block = sec * 8 + dev // 2
    masked = jnp.where(jnp.any(parent_pivots == row_block), jnp.zeros_like(share), share)
    masked = after(masked, rings[0].marks[0])
    pairs = [(s * 16 + d, (d % 8) * 16 + 2 * s + d // 8) for s in range(8) for d in range(16)]
    moved = lax.ppermute(masked, AXES, pairs)
    moved = after(moved, rings[0].marks[1])
    both = ordered_pair(h, moved, shift(moved, "h", 1))
    both = after(both, rings[0].marks[2])
    ring = ordered_ring(y, [both, shift(both, "y", -1), shift(both, "y", 2), shift(both, "y", 1)])
    column_factor = ring.transpose(1, 0, 2, 3).reshape(512, 1024)

    both_z = ordered_pair(z, share, shift(share, "z", 1))
    copies = jnp.broadcast_to(after(both_z, rings[1].marks[0]), (8, 2, 64, 1024))
    copies = lax.all_to_all(copies, ("x", "c"), split_axis=0, concat_axis=0, tiled=True)
    parent_factor = copies.reshape(4, 2, 2, 64, 1024).transpose(0, 2, 1, 3, 4).reshape(1024, 1024)

    my_blocks = sec * 8 + jnp.arange(8, dtype=jnp.int32)
    is_pivot = jnp.any(parent_pivots[None, :] == my_blocks[:, None], axis=1)
    row_pivot = jnp.repeat(is_pivot, BLK)
    update = lax.dot_general(
        parent_factor, column_factor, (((1,), (1,)), ((), ())), preferred_element_type=F32
    )
    update = jnp.where(row_pivot[:, None], jnp.zeros_like(update), update)
    update = lax.optimization_barrier(update)
    parent_factor = jnp.where(parent_pivots[0] < 0, jnp.zeros_like(parent_factor), parent_factor)
    return assembled - update, parent_factor


def solution(mesh):
    fine = Mesh(mesh.devices.reshape(tuple(SIZE[a] for a in AXES)), AXES)
    sec, dev = ("h", "y"), ("x", "z", "c")
    placed = (P(sec, dev, None), P(sec, None, None), P(), P(sec, dev), P(), P())
    return jax.shard_map(
        local,
        mesh=fine,
        in_specs=placed,
        out_specs=(P(sec, dev), P(sec, None)),
        check_vma=False,
    )
```

```python
import functools

import jax
import jax.numpy as jnp
from jax import lax
from jax.experimental import pallas as pl
from jax.experimental.pallas import tpu as pltpu
from jax.sharding import Mesh
from jax.sharding import PartitionSpec as P

BLK = 128
PORD = 8192
PIV = 2048
KH = PIV // 2
OWN = 384
STEP = 12
BF = jnp.bfloat16
F32 = jnp.float32
VMEM_LIMIT = 60 * 2**20
SMEM_SPEC = pl.BlockSpec(memory_space=pltpu.SMEM)
ANY_SPEC = pl.BlockSpec(memory_space=pl.ANY)
SIZE = {"h": 2, "y": 4, "x": 4, "z": 2, "c": 2}
AXES = ("h", "y", "x", "z", "c")
def shift(array, axis, step):
    size = SIZE[axis]
    return lax.ppermute(array, axis, [(i, (i + step) % size) for i in range(size)])


def mirrored(array, axis, step):
    size = SIZE[axis]
    pairs = [
        (i * 2 + core, (i + (step if core == 0 else -step)) % size * 2 + core)
        for i in range(size)
        for core in range(2)
    ]
    return lax.ppermute(array, (axis, "c"), pairs)


def after(value, *earlier):
    return lax.optimization_barrier((value,) + earlier)[0]


def factor_kernel(panel, inverse, out, held, sems):
    width = 512
    for j in range(PIV // width):
        deep = (j + 1) * width
        pltpu.make_async_copy(
            inverse.at[0, pl.ds(0, deep), pl.ds(j * width, width)],
            held.at[pl.ds(0, deep), pl.ds(j * width, width)],
            sems.at[j],
        ).start()
    for j in range(PIV // width):
        deep = (j + 1) * width
        pltpu.make_async_copy(
            inverse.at[0, pl.ds(0, deep), pl.ds(j * width, width)],
            held.at[pl.ds(0, deep), pl.ds(j * width, width)],
            sems.at[j],
        ).wait()
        out[:, j * width : deep] = jnp.dot(
            panel[0, :, :deep], held[:deep, j * width : deep], preferred_element_type=F32
        ).astype(BF)


def factor(panel, inverse):
    vmem = pl.BlockSpec(memory_space=pltpu.VMEM)
    return pl.pallas_call(
        factor_kernel,
        out_shape=jax.ShapeDtypeStruct((OWN, PIV), BF),
        in_specs=[vmem, ANY_SPEC],
        out_specs=vmem,
        scratch_shapes=[pltpu.VMEM((PIV, PIV), BF), pltpu.SemaphoreType.DMA((4,))],
        compiler_params=pltpu.CompilerParams(vmem_limit_bytes=VMEM_LIMIT),
        cost_estimate=pl.CostEstimate(
            flops=2_000_000_000, bytes_accessed=8_000_000, transcendentals=0
        ),
    )(panel, inverse)


def gather_rows(own, ready):
    w = mirrored(own, "x", 1)
    e = mirrored(own, "x", -1)
    z = shift(own, "z", 1)
    core = shift(own, "c", 1)
    w, e, z, core, ready = lax.optimization_barrier((w, e, z, core, ready))
    b = shift(w, "z", 1)
    q = mirrored(w, "x", 1)
    a = mirrored(z, "x", -1)
    cross = [shift(v, "c", 1) for v in (w, e)]
    q, a, b, cross = lax.optimization_barrier((q, a, b, cross))
    r = mirrored(b, "x", 1)
    last = cross + [shift(v, "c", 1) for v in (z, q, a, b, r)]
    pieces, first = [], 0
    for array in (own, w, e, z, q, a, b, r, core, *last):
        pieces.append((array, first, array.shape[0] // BLK))
        first += array.shape[0] // BLK
    return pieces, ready


PLACE = [[0, 3], [2, 5], [4, 7], [1, 6]]


def fetch(ins, pieces, block, dst, sem, first_row=0, count=BLK):
    for ref, (first, blocks) in zip(ins, pieces):

        @pl.when((block >= first) & (block < first + blocks))
        def _(ref=ref, first=first):
            row = pl.multiple_of((block - first) * BLK + first_row, 64)
            pltpu.make_async_copy(ref.at[pl.ds(row, count), :], dst, sem).start()


def fetched(ins, block, dst, sem, count=BLK):
    @pl.when(block < 0)
    def _():
        dst[...] = jnp.zeros((count, PIV), BF)

    @pl.when(block >= 0)
    def _():
        pltpu.make_async_copy(ins[0].at[pl.ds(0, count), :], dst, sem).wait()


def main_kernel(pieces, dest, chosen, *refs):
    n = len(pieces)
    ins, outs = refs[:n], refs[n : n + 16]
    rows, cols, turned, placed, sem_in, sem_sel, sem_out = refs[n + 16 :]

    for m in range(4):
        fetch(ins, pieces, chosen[m], cols.at[pl.ds(m * BLK, BLK), :], sem_sel.at[m])

    def arrival(i):
        first, blocks = pieces[i]
        return pltpu.make_async_copy(
            ins[i], rows.at[pl.ds(first * BLK, blocks * BLK), :], sem_in.at[i]
        )

    early = 4
    for i in range(early):
        arrival(i).start()

    @pl.loop(0, PORD // 256)
    def _(i):
        for half in range(2):
            placed[half, pl.ds(pl.multiple_of(i * 256, 256), 256), :] = jnp.zeros((256, 256), BF)

    for m in range(4):
        fetched(ins, chosen[m], cols.at[pl.ds(m * BLK, BLK), :], sem_sel.at[m])
    for i in range(early, n):
        arrival(i).start()

    turned[...] = cols[...].T

    def multiply(block, count):
        product = jnp.dot(
            rows[pl.ds(block * BLK, count * BLK), :], turned[...], preferred_element_type=F32
        )
        for b in range(count):
            at = pl.multiple_of(dest[block + b] * BLK, BLK)
            result = (-product[b * BLK : (b + 1) * BLK]).astype(BF)
            placed[0, pl.ds(at, BLK), :] = result[:, :256]
            placed[1, pl.ds(at, BLK), :] = result[:, 256:]

    done, at = 0, 0
    for i in range(n):
        arrival(i).wait()
        done += pieces[i][1]
        if (done - at) % STEP == 0:

            @pl.loop(0, (done - at) // STEP)
            def _(k, at=at):
                multiply(at + k * STEP, STEP)

            at = done

    def leaving(i):
        return pltpu.make_async_copy(
            placed.at[i % 2, pl.ds((i // 2) * 1024, 1024), :], outs[i], sem_out.at[i]
        )

    for i in range(16):
        leaving(i).start()
    for i in range(16):
        leaving(i).wait()


def main_parts(pieces, dest, chosen):
    arrays = [p[0] for p in pieces]
    n = len(arrays)
    outs = pl.pallas_call(
        functools.partial(main_kernel, [p[1:] for p in pieces]),
        out_shape=[jax.ShapeDtypeStruct((1024, 256), BF)] * 16,
        in_specs=[SMEM_SPEC] * 2 + [ANY_SPEC] * n,
        out_specs=[ANY_SPEC] * 16,
        scratch_shapes=[
            pltpu.VMEM((6144, PIV), BF),
            pltpu.VMEM((512, PIV), BF),
            pltpu.VMEM((PIV, 512), BF),
            pltpu.VMEM((2, PORD, 256), BF),
            pltpu.SemaphoreType.DMA((n,)),
            pltpu.SemaphoreType.DMA((4,)),
            pltpu.SemaphoreType.DMA((16,)),
        ],
        compiler_params=pltpu.CompilerParams(vmem_limit_bytes=VMEM_LIMIT),
        cost_estimate=pl.CostEstimate(
            flops=20_000_000_000, bytes_accessed=36_000_000, transcendentals=0
        ),
    )(dest, chosen, *arrays)
    return [[[outs[(dh * 4 + dy) * 2 + k] for k in range(2)] for dy in range(4)] for dh in range(2)]


def panel_kernel(pieces, pan_rows, pan_cols, offset, *refs):
    n = len(pieces)
    ins, out = refs[:n], refs[n]
    left, right, sem_left, sem_right = refs[n + 1 :]
    to_left = lambda q: left.at[pl.ds(q * 64, 64), :]
    to_right = lambda q: right.at[pl.ds(q * BLK, BLK), :]
    for q in range(8):
        fetch(ins, pieces, pan_rows[q], to_left(q), sem_left.at[q], offset[0], 64)
        fetch(ins, pieces, pan_cols[q], to_right(q), sem_right.at[q])
    for q in range(8):
        fetched(ins, pan_rows[q], to_left(q), sem_left.at[q], 64)
    for q in range(8):
        fetched(ins, pan_cols[q], to_right(q), sem_right.at[q])

    for part in range(4):
        product = lax.dot_general(
            left[...],
            right[pl.ds(part * 256, 256), :],
            (((1,), (1,)), ((), ())),
            preferred_element_type=F32,
        )
        out[:, part * 256 : (part + 1) * 256] = (-product).astype(BF)


def panel_parts(pieces, pan_rows, pan_cols, offset):
    arrays = [p[0] for p in pieces]
    n = len(arrays)
    return pl.pallas_call(
        functools.partial(panel_kernel, [p[1:] for p in pieces]),
        out_shape=jax.ShapeDtypeStruct((512, 1024), BF),
        in_specs=[SMEM_SPEC] * 3 + [ANY_SPEC] * n,
        out_specs=pl.BlockSpec(memory_space=pltpu.VMEM),
        scratch_shapes=[
            pltpu.VMEM((512, PIV), BF),
            pltpu.VMEM((1024, PIV), BF),
            pltpu.SemaphoreType.DMA((8,)),
            pltpu.SemaphoreType.DMA((8,)),
        ],
        compiler_params=pltpu.CompilerParams(vmem_limit_bytes=VMEM_LIMIT),
        cost_estimate=pl.CostEstimate(
            flops=2_200_000_000, bytes_accessed=8_000_000, transcendentals=0
        ),
    )(pan_rows, pan_cols, offset, *arrays)


class Ring:
    def __init__(self, term, gate=None):
        carried = term(3).astype(BF)
        if gate is not None:
            carried = after(carried, gate)
        self.marks = []
        for k in (2, 1, 0):
            moved = mirrored(carried, "y", 1)
            self.marks.append(moved)
            self.total = term(k).astype(F32) + moved.astype(F32)
            carried = self.total.astype(BF)


def pick(bit, when_zero, when_one):
    return jnp.where(bit == 0, when_zero, when_one)


def ordered_pair(bit, own, other):
    return jnp.stack([pick(bit, own, other), pick(bit, other, own)])


def ordered_ring(at, parts):
    twice = jnp.stack(list(parts) + list(parts))
    return lax.dynamic_slice_in_dim(twice, (4 - at) % 4, 4, 0)


def front_kernel(pivots, place, front, keep, send, zeros, sems):
    zeros[...] = jnp.zeros_like(zeros)
    for r in range(8):
        columns = pl.ds(r * BLK, BLK)
        local_block = pivots[r] - place[0] * 4
        mine = (local_block >= 0) & (local_block < 4)
        for k, out in enumerate((keep, send)):

            @pl.when(mine)
            def _(k=k, out=out, columns=columns, r=r):
                pltpu.make_async_copy(
                    front.at[:, place[1] ^ k, :, pl.ds(pl.multiple_of(local_block * BLK, BLK), BLK)],
                    out.at[:, :, columns],
                    sems.at[r, k],
                ).start()

            @pl.when(jnp.logical_not(mine))
            def _(k=k, out=out, columns=columns, r=r):
                pltpu.make_async_copy(zeros, out.at[:, :, columns], sems.at[r, k]).start()

    for r in range(8):
        for k, out in enumerate((keep, send)):
            pltpu.make_async_copy(zeros, out.at[:, :, pl.ds(r * BLK, BLK)], sems.at[r, k]).wait()


def front_pick(pivots, place, front):
    return pl.pallas_call(
        front_kernel,
        out_shape=[jax.ShapeDtypeStruct((8, 64, 1024), BF)] * 2,
        in_specs=[SMEM_SPEC] * 2 + [ANY_SPEC],
        out_specs=[ANY_SPEC] * 2,
        scratch_shapes=[pltpu.VMEM((8, 64, BLK), BF), pltpu.SemaphoreType.DMA((8, 2))],
        compiler_params=pltpu.CompilerParams(vmem_limit_bytes=VMEM_LIMIT),
    )(pivots, place, front.reshape(8, 2, 64, 512))


def local(child_panel, child_inverse, child_map, parent_front, parent_inverse, parent_pivots):
    h, y, x, z, c = (lax.axis_index(a) for a in AXES)
    sec = h * 4 + y
    dev = x * 4 + z * 2 + c

    my_map = lax.dynamic_index_in_dim(child_map, sec, 0, keepdims=False)
    place_table = jnp.array(PLACE, jnp.int32)
    child = jnp.arange(48, dtype=jnp.int32)
    owner = child // 3
    place = place_table[
        (owner // 4 - x) * (1 - 2 * (owner % 2)) % 4, (owner // 2 % 2) ^ z
    ]
    position = ((owner % 2) ^ c) * 24 + place * 3 + child % 3
    parent_row = my_map // 8
    slot = (((parent_row // 4) ^ h) * 4 + (parent_row % 4 - y) * (1 - 2 * c) % 4) * 8 + my_map % 8
    dest = jnp.sum(
        jnp.where(position[None, :] == child[:, None], slot[None, :], 0), axis=1, dtype=jnp.int32
    )

    def find(targets):
        hit = my_map[None, :] == targets[:, None]
        return jnp.sum(jnp.where(hit, position[None, :] + 1, 0), axis=1, dtype=jnp.int32) - 1

    chosen = find(dev * 4 + jnp.arange(4, dtype=jnp.int32))
    pan_rows = find(jnp.arange(8, dtype=jnp.int32) * 8 + dev // 2)
    pan_cols = find(parent_pivots)
    offset = (dev % 2 * 64).astype(jnp.int32).reshape(1)

    keep, send = front_pick(parent_pivots, jnp.stack([dev, c]).astype(jnp.int32), parent_front)
    front = (keep + shift(send, "c", 1)).reshape(4, 2, 64, 1024)
    front_x = [lax.dynamic_index_in_dim(front, (x + k) % 4, 0, keepdims=False) for k in range(4)]

    pieces, ready = gather_rows(
        factor(child_panel, child_inverse), (dest, chosen, pan_rows, pan_cols, offset, front_x)
    )
    dest, chosen, pan_rows, pan_cols, offset, front_x = ready

    pan = panel_parts(pieces, pan_rows, pan_cols, offset)
    arrived = lax.all_to_all(
        pan.reshape(8, 64, 1024), ("h", "y"), split_axis=0, concat_axis=0, tiled=True
    )
    main = main_parts(pieces, dest, chosen)

    front_x = [after(v, pan) for v in front_x]
    front_z = (
        front_x[0]
        + shift(front_x[1], "x", 1)
        + shift(front_x[3], "x", -1)
        + shift(front_x[2], "x", 2)
    )
    front_rows = pick(z, front_z[0], front_z[1]) + shift(pick(z, front_z[1], front_z[0]), "z", 1)

    arrived, main = lax.optimization_barrier((arrived, main))
    pan_rows_f = arrived.astype(F32).sum(axis=0) + front_rows.astype(F32)
    share = jnp.dot(pan_rows_f.astype(BF), parent_inverse, preferred_element_type=F32).astype(BF)

    rings = []
    for d in (1, 0):
        for half in range(2):
            rings.append(
                Ring(
                    lambda k: main[d][k][half],
                    None if d == 1 else rings[half].marks[0],
                )
            )
    far = [shift(ring.total.astype(BF), "h", 1).astype(F32) for ring in rings[:2]]
    near = jnp.concatenate([rings[2].total + far[0], rings[3].total + far[1]], axis=1)
    assembled = parent_front.astype(F32) + near

    row_block = sec * 8 + dev // 2
    masked = jnp.where(jnp.any(parent_pivots == row_block), jnp.zeros_like(share), share)
    masked = after(masked, rings[0].marks[0])
    pairs = [(s * 16 + d, (d % 8) * 16 + 2 * s + d // 8) for s in range(8) for d in range(16)]
    moved = lax.ppermute(masked, AXES, pairs)
    both = ordered_pair(h, moved, shift(moved, "h", 1))
    share = after(share, both)
    both = after(both, rings[1].marks[1])
    ring = ordered_ring(y, [both, shift(both, "y", -1), shift(both, "y", 2), shift(both, "y", 1)])
    column_factor = ring.transpose(1, 0, 2, 3).reshape(512, 1024)

    copies = jnp.broadcast_to(share, (16, 64, 1024))
    parent_factor = lax.all_to_all(
        copies, ("x", "z", "c"), split_axis=0, concat_axis=0, tiled=True
    ).reshape(1024, 1024)

    my_blocks = sec * 8 + jnp.arange(8, dtype=jnp.int32)
    is_pivot = jnp.any(parent_pivots[None, :] == my_blocks[:, None], axis=1)
    row_pivot = jnp.repeat(is_pivot, BLK)
    trailing = jnp.where(row_pivot[:, None], jnp.zeros_like(parent_factor), parent_factor)
    update = lax.dot_general(
        trailing, column_factor, (((1,), (1,)), ((), ())), preferred_element_type=F32
    )
    update = lax.optimization_barrier(update)
    parent_factor = jnp.where(parent_pivots[0] < 0, jnp.zeros_like(parent_factor), parent_factor)
    return assembled - update, parent_factor


def solution(mesh):
    fine = Mesh(mesh.devices.reshape(tuple(SIZE[a] for a in AXES)), AXES)
    sec, dev = ("h", "y"), ("x", "z", "c")
    placed = (P(sec, dev, None), P(sec, None, None), P(), P(sec, dev), P(), P())
    return jax.shard_map(
        local,
        mesh=fine,
        in_specs=placed,
        out_specs=(P(sec, dev), P(sec, None)),
        check_vma=False,
    )
```

```python
import functools

import jax
import jax.numpy as jnp
from jax import lax
from jax.experimental import pallas as pl
from jax.experimental.pallas import tpu as pltpu
from jax.sharding import Mesh
from jax.sharding import PartitionSpec as P

BLK = 128
PORD = 8192
PIV = 2048
KH = PIV // 2
OWN = 384
STEP = 12
BF = jnp.bfloat16
F32 = jnp.float32
VMEM_LIMIT = 60 * 2**20
SMEM_SPEC = pl.BlockSpec(memory_space=pltpu.SMEM)
ANY_SPEC = pl.BlockSpec(memory_space=pl.ANY)
SIZE = {"h": 2, "y": 4, "x": 4, "z": 2, "c": 2}
AXES = ("h", "y", "x", "z", "c")
def shift(array, axis, step):
    size = SIZE[axis]
    return lax.ppermute(array, axis, [(i, (i + step) % size) for i in range(size)])


def mirrored(array, axis, step):
    size = SIZE[axis]
    pairs = [
        (i * 2 + core, (i + (step if core == 0 else -step)) % size * 2 + core)
        for i in range(size)
        for core in range(2)
    ]
    return lax.ppermute(array, (axis, "c"), pairs)


def after(value, *earlier):
    return lax.optimization_barrier((value,) + earlier)[0]


def factor_kernel(panel, inverse, out, held, sems):
    width = 512
    for j in range(PIV // width):
        deep = (j + 1) * width
        pltpu.make_async_copy(
            inverse.at[0, pl.ds(0, deep), pl.ds(j * width, width)],
            held.at[pl.ds(0, deep), pl.ds(j * width, width)],
            sems.at[j],
        ).start()
    for j in range(PIV // width):
        deep = (j + 1) * width
        pltpu.make_async_copy(
            inverse.at[0, pl.ds(0, deep), pl.ds(j * width, width)],
            held.at[pl.ds(0, deep), pl.ds(j * width, width)],
            sems.at[j],
        ).wait()
        out[:, j * width : deep] = jnp.dot(
            panel[0, :, :deep], held[:deep, j * width : deep], preferred_element_type=F32
        ).astype(BF)


def factor(panel, inverse):
    vmem = pl.BlockSpec(memory_space=pltpu.VMEM)
    return pl.pallas_call(
        factor_kernel,
        out_shape=jax.ShapeDtypeStruct((OWN, PIV), BF),
        in_specs=[vmem, ANY_SPEC],
        out_specs=vmem,
        scratch_shapes=[pltpu.VMEM((PIV, PIV), BF), pltpu.SemaphoreType.DMA((4,))],
        compiler_params=pltpu.CompilerParams(vmem_limit_bytes=VMEM_LIMIT),
        cost_estimate=pl.CostEstimate(
            flops=2_000_000_000, bytes_accessed=8_000_000, transcendentals=0
        ),
    )(panel, inverse)


def gather_rows(own, ready):
    w = mirrored(own, "x", 1)
    e = mirrored(own, "x", -1)
    z = shift(own, "z", 1)
    core = shift(own, "c", 1)
    w, e, z, core, ready = lax.optimization_barrier((w, e, z, core, ready))
    b = shift(w, "z", 1)
    q = mirrored(w, "x", 1)
    a = mirrored(z, "x", -1)
    cross = [shift(v, "c", 1) for v in (w, e)]
    q, a, b, cross = lax.optimization_barrier((q, a, b, cross))
    r = mirrored(b, "x", 1)
    last = cross + [shift(v, "c", 1) for v in (z, q, a, b, r)]
    pieces, first = [], 0
    for array in (own, w, e, z, q, a, b, r, core, *last):
        pieces.append((array, first, array.shape[0] // BLK))
        first += array.shape[0] // BLK
    return pieces, ready


PLACE = [[0, 3], [2, 5], [4, 7], [1, 6]]


def fetch(ins, pieces, block, dst, sem, first_row=0, count=BLK):
    for ref, (first, blocks) in zip(ins, pieces):

        @pl.when((block >= first) & (block < first + blocks))
        def _(ref=ref, first=first):
            row = pl.multiple_of((block - first) * BLK + first_row, 64)
            pltpu.make_async_copy(ref.at[pl.ds(row, count), :], dst, sem).start()


def fetched(ins, block, dst, sem, count=BLK):
    @pl.when(block < 0)
    def _():
        dst[...] = jnp.zeros((count, PIV), BF)

    @pl.when(block >= 0)
    def _():
        pltpu.make_async_copy(ins[0].at[pl.ds(0, count), :], dst, sem).wait()


def main_kernel(pieces, dest, chosen, *refs):
    n = len(pieces)
    ins, outs = refs[:n], refs[n : n + 16]
    rows, cols, turned, placed, sem_in, sem_sel, sem_out = refs[n + 16 :]

    for m in range(4):
        fetch(ins, pieces, chosen[m], cols.at[pl.ds(m * BLK, BLK), :], sem_sel.at[m])

    def arrival(i):
        first, blocks = pieces[i]
        return pltpu.make_async_copy(
            ins[i], rows.at[pl.ds(first * BLK, blocks * BLK), :], sem_in.at[i]
        )

    early = 4
    for i in range(early):
        arrival(i).start()

    @pl.loop(0, PORD // 256)
    def _(i):
        for half in range(2):
            placed[half, pl.ds(pl.multiple_of(i * 256, 256), 256), :] = jnp.zeros((256, 256), BF)

    for m in range(4):
        fetched(ins, chosen[m], cols.at[pl.ds(m * BLK, BLK), :], sem_sel.at[m])
    for i in range(early, n):
        arrival(i).start()

    turned[...] = cols[...].T

    def multiply(block, count):
        product = jnp.dot(
            rows[pl.ds(block * BLK, count * BLK), :], turned[...], preferred_element_type=F32
        )
        for b in range(count):
            at = pl.multiple_of(dest[block + b] * BLK, BLK)
            result = (-product[b * BLK : (b + 1) * BLK]).astype(BF)
            placed[0, pl.ds(at, BLK), :] = result[:, :256]
            placed[1, pl.ds(at, BLK), :] = result[:, 256:]

    done, at = 0, 0
    for i in range(n):
        arrival(i).wait()
        done += pieces[i][1]
        if (done - at) % STEP == 0:

            @pl.loop(0, (done - at) // STEP)
            def _(k, at=at):
                multiply(at + k * STEP, STEP)

            at = done

    def leaving(i):
        return pltpu.make_async_copy(
            placed.at[i % 2, pl.ds((i // 2) * 1024, 1024), :], outs[i], sem_out.at[i]
        )

    for i in range(16):
        leaving(i).start()
    for i in range(16):
        leaving(i).wait()


def main_parts(pieces, dest, chosen):
    arrays = [p[0] for p in pieces]
    n = len(arrays)
    outs = pl.pallas_call(
        functools.partial(main_kernel, [p[1:] for p in pieces]),
        out_shape=[jax.ShapeDtypeStruct((1024, 256), BF)] * 16,
        in_specs=[SMEM_SPEC] * 2 + [ANY_SPEC] * n,
        out_specs=[ANY_SPEC] * 16,
        scratch_shapes=[
            pltpu.VMEM((6144, PIV), BF),
            pltpu.VMEM((512, PIV), BF),
            pltpu.VMEM((PIV, 512), BF),
            pltpu.VMEM((2, PORD, 256), BF),
            pltpu.SemaphoreType.DMA((n,)),
            pltpu.SemaphoreType.DMA((4,)),
            pltpu.SemaphoreType.DMA((16,)),
        ],
        compiler_params=pltpu.CompilerParams(vmem_limit_bytes=VMEM_LIMIT),
        cost_estimate=pl.CostEstimate(
            flops=20_000_000_000, bytes_accessed=36_000_000, transcendentals=0
        ),
    )(dest, chosen, *arrays)
    return [[[outs[(dh * 4 + dy) * 2 + k] for k in range(2)] for dy in range(4)] for dh in range(2)]


def panel_kernel(pieces, pan_rows, pan_cols, offset, *refs):
    n = len(pieces)
    ins, out = refs[:n], refs[n]
    left, right, sem_left, sem_right = refs[n + 1 :]
    to_left = lambda q: left.at[pl.ds(q * 64, 64), :]
    to_right = lambda q: right.at[pl.ds(q * BLK, BLK), :]
    for q in range(8):
        fetch(ins, pieces, pan_rows[q], to_left(q), sem_left.at[q], offset[0], 64)
        fetch(ins, pieces, pan_cols[q], to_right(q), sem_right.at[q])
    for q in range(8):
        fetched(ins, pan_rows[q], to_left(q), sem_left.at[q], 64)
    for q in range(8):
        fetched(ins, pan_cols[q], to_right(q), sem_right.at[q])

    for part in range(4):
        product = lax.dot_general(
            left[...],
            right[pl.ds(part * 256, 256), :],
            (((1,), (1,)), ((), ())),
            preferred_element_type=F32,
        )
        out[:, part * 256 : (part + 1) * 256] = (-product).astype(BF)


def panel_parts(pieces, pan_rows, pan_cols, offset):
    arrays = [p[0] for p in pieces]
    n = len(arrays)
    return pl.pallas_call(
        functools.partial(panel_kernel, [p[1:] for p in pieces]),
        out_shape=jax.ShapeDtypeStruct((512, 1024), BF),
        in_specs=[SMEM_SPEC] * 3 + [ANY_SPEC] * n,
        out_specs=pl.BlockSpec(memory_space=pltpu.VMEM),
        scratch_shapes=[
            pltpu.VMEM((512, PIV), BF),
            pltpu.VMEM((1024, PIV), BF),
            pltpu.SemaphoreType.DMA((8,)),
            pltpu.SemaphoreType.DMA((8,)),
        ],
        compiler_params=pltpu.CompilerParams(vmem_limit_bytes=VMEM_LIMIT),
        cost_estimate=pl.CostEstimate(
            flops=2_200_000_000, bytes_accessed=8_000_000, transcendentals=0
        ),
    )(pan_rows, pan_cols, offset, *arrays)


class Ring:
    def __init__(self, term, gate=None):
        carried = term(3).astype(BF)
        if gate is not None:
            carried = after(carried, gate)
        self.marks = []
        for k in (2, 1, 0):
            moved = mirrored(carried, "y", 1)
            self.marks.append(moved)
            self.total = term(k).astype(F32) + moved.astype(F32)
            carried = self.total.astype(BF)


def pick(bit, when_zero, when_one):
    return jnp.where(bit == 0, when_zero, when_one)


def ordered_pair(bit, own, other):
    return jnp.stack([pick(bit, own, other), pick(bit, other, own)])


def ordered_ring(at, parts):
    twice = jnp.stack(list(parts) + list(parts))
    return lax.dynamic_slice_in_dim(twice, (4 - at) % 4, 4, 0)


def front_kernel(pivots, place, front, keep, send, zeros, sems):
    zeros[...] = jnp.zeros_like(zeros)
    for r in range(8):
        columns = pl.ds(r * BLK, BLK)
        local_block = pivots[r] - place[0] * 4
        mine = (local_block >= 0) & (local_block < 4)
        for k, out in enumerate((keep, send)):

            @pl.when(mine)
            def _(k=k, out=out, columns=columns, r=r):
                pltpu.make_async_copy(
                    front.at[:, place[1] ^ k, :, pl.ds(pl.multiple_of(local_block * BLK, BLK), BLK)],
                    out.at[:, :, columns],
                    sems.at[r, k],
                ).start()

            @pl.when(jnp.logical_not(mine))
            def _(k=k, out=out, columns=columns, r=r):
                pltpu.make_async_copy(zeros, out.at[:, :, columns], sems.at[r, k]).start()

    for r in range(8):
        for k, out in enumerate((keep, send)):
            pltpu.make_async_copy(zeros, out.at[:, :, pl.ds(r * BLK, BLK)], sems.at[r, k]).wait()


def front_pick(pivots, place, front):
    return pl.pallas_call(
        front_kernel,
        out_shape=[jax.ShapeDtypeStruct((8, 64, 1024), BF)] * 2,
        in_specs=[SMEM_SPEC] * 2 + [ANY_SPEC],
        out_specs=[ANY_SPEC] * 2,
        scratch_shapes=[pltpu.VMEM((8, 64, BLK), BF), pltpu.SemaphoreType.DMA((8, 2))],
        compiler_params=pltpu.CompilerParams(vmem_limit_bytes=VMEM_LIMIT),
    )(pivots, place, front.reshape(8, 2, 64, 512))


def local(child_panel, child_inverse, child_map, parent_front, parent_inverse, parent_pivots):
    h, y, x, z, c = (lax.axis_index(a) for a in AXES)
    sec = h * 4 + y
    dev = x * 4 + z * 2 + c

    my_map = lax.dynamic_index_in_dim(child_map, sec, 0, keepdims=False)
    place_table = jnp.array(PLACE, jnp.int32)
    child = jnp.arange(48, dtype=jnp.int32)
    owner = child // 3
    place = place_table[
        (owner // 4 - x) * (1 - 2 * (owner % 2)) % 4, (owner // 2 % 2) ^ z
    ]
    position = ((owner % 2) ^ c) * 24 + place * 3 + child % 3
    parent_row = my_map // 8
    slot = (((parent_row // 4) ^ h) * 4 + (parent_row % 4 - y) * (1 - 2 * c) % 4) * 8 + my_map % 8
    dest = jnp.sum(
        jnp.where(position[None, :] == child[:, None], slot[None, :], 0), axis=1, dtype=jnp.int32
    )

    def find(targets):
        hit = my_map[None, :] == targets[:, None]
        return jnp.sum(jnp.where(hit, position[None, :] + 1, 0), axis=1, dtype=jnp.int32) - 1

    chosen = find(dev * 4 + jnp.arange(4, dtype=jnp.int32))
    pan_rows = find(jnp.arange(8, dtype=jnp.int32) * 8 + dev // 2)
    pan_cols = find(parent_pivots)
    offset = (dev % 2 * 64).astype(jnp.int32).reshape(1)

    keep, send = front_pick(parent_pivots, jnp.stack([dev, c]).astype(jnp.int32), parent_front)
    front = (keep + shift(send, "c", 1)).reshape(4, 2, 64, 1024)
    front_x = [lax.dynamic_index_in_dim(front, (x + k) % 4, 0, keepdims=False) for k in range(4)]

    pieces, ready = gather_rows(
        factor(child_panel, child_inverse), (dest, chosen, pan_rows, pan_cols, offset, front_x)
    )
    dest, chosen, pan_rows, pan_cols, offset, front_x = ready

    pan = panel_parts(pieces, pan_rows, pan_cols, offset)
    arrived = lax.all_to_all(
        pan.reshape(8, 64, 1024), ("h", "y"), split_axis=0, concat_axis=0, tiled=True
    )
    main = main_parts(pieces, dest, chosen)

    front_x = [after(v, pan) for v in front_x]
    front_z = (
        front_x[0]
        + shift(front_x[1], "x", 1)
        + shift(front_x[3], "x", -1)
        + shift(front_x[2], "x", 2)
    )
    front_rows = pick(z, front_z[0], front_z[1]) + shift(pick(z, front_z[1], front_z[0]), "z", 1)

    arrived, main = lax.optimization_barrier((arrived, main))
    pan_rows_f = arrived.astype(F32).sum(axis=0) + front_rows.astype(F32)
    share = jnp.dot(pan_rows_f.astype(BF), parent_inverse, preferred_element_type=F32).astype(BF)

    rings = []
    for d in (1, 0):
        for half in range(2):
            rings.append(
                Ring(
                    lambda k: main[d][k][half],
                    None if d == 1 else rings[half].marks[0],
                )
            )
    far = [shift(ring.total.astype(BF), "h", 1).astype(F32) for ring in rings[:2]]
    near = jnp.concatenate([rings[2].total + far[0], rings[3].total + far[1]], axis=1)
    assembled = parent_front.astype(F32) + near

    row_block = sec * 8 + dev // 2
    masked = jnp.where(jnp.any(parent_pivots == row_block), jnp.zeros_like(share), share)
    masked = after(masked, rings[0].marks[0])
    pairs = [(s * 16 + d, (d % 8) * 16 + 2 * s + d // 8) for s in range(8) for d in range(16)]
    moved = lax.ppermute(masked, AXES, pairs)
    both = ordered_pair(h, moved, shift(moved, "h", 1))
    share = after(share, both)
    both = after(both, rings[1].marks[2])
    ring = ordered_ring(y, [both, shift(both, "y", -1), shift(both, "y", 2), shift(both, "y", 1)])
    column_factor = ring.transpose(1, 0, 2, 3).reshape(512, 1024)

    copies = jnp.broadcast_to(share, (16, 64, 1024))
    parent_factor = lax.all_to_all(
        copies, ("x", "z", "c"), split_axis=0, concat_axis=0, tiled=True
    ).reshape(1024, 1024)

    my_blocks = sec * 8 + jnp.arange(8, dtype=jnp.int32)
    is_pivot = jnp.any(parent_pivots[None, :] == my_blocks[:, None], axis=1)
    row_pivot = jnp.repeat(is_pivot, BLK)
    trailing = jnp.where(row_pivot[:, None], jnp.zeros_like(parent_factor), parent_factor)
    update = lax.dot_general(
        trailing, column_factor, (((1,), (1,)), ((), ())), preferred_element_type=F32
    )
    update = lax.optimization_barrier(update)
    parent_factor = jnp.where(parent_pivots[0] < 0, jnp.zeros_like(parent_factor), parent_factor)
    return assembled - update, parent_factor


def solution(mesh):
    fine = Mesh(mesh.devices.reshape(tuple(SIZE[a] for a in AXES)), AXES)
    sec, dev = ("h", "y"), ("x", "z", "c")
    placed = (P(sec, dev, None), P(sec, None, None), P(), P(sec, dev), P(), P())
    return jax.shard_map(
        local,
        mesh=fine,
        in_specs=placed,
        out_specs=(P(sec, dev), P(sec, None)),
        check_vma=False,
    )
```

```python
import functools

import jax
import jax.numpy as jnp
from jax import lax
from jax.experimental import pallas as pl
from jax.experimental.pallas import tpu as pltpu
from jax.sharding import Mesh
from jax.sharding import PartitionSpec as P

BLK = 128
PORD = 8192
PIV = 2048
KH = PIV // 2
OWN = 384
STEP = 12
BF = jnp.bfloat16
F32 = jnp.float32
VMEM_LIMIT = 60 * 2**20
SMEM_SPEC = pl.BlockSpec(memory_space=pltpu.SMEM)
ANY_SPEC = pl.BlockSpec(memory_space=pl.ANY)
SIZE = {"h": 2, "y": 4, "x": 4, "z": 2, "c": 2}
AXES = ("h", "y", "x", "z", "c")
def shift(array, axis, step):
    size = SIZE[axis]
    return lax.ppermute(array, axis, [(i, (i + step) % size) for i in range(size)])


def mirrored(array, axis, step):
    size = SIZE[axis]
    pairs = [
        (i * 2 + core, (i + (step if core == 0 else -step)) % size * 2 + core)
        for i in range(size)
        for core in range(2)
    ]
    return lax.ppermute(array, (axis, "c"), pairs)


def after(value, *earlier):
    return lax.optimization_barrier((value,) + earlier)[0]


def factor_kernel(panel, inverse, out, held, sems):
    width = 512
    for j in range(PIV // width):
        deep = (j + 1) * width
        pltpu.make_async_copy(
            inverse.at[0, pl.ds(0, deep), pl.ds(j * width, width)],
            held.at[pl.ds(0, deep), pl.ds(j * width, width)],
            sems.at[j],
        ).start()
    for j in range(PIV // width):
        deep = (j + 1) * width
        pltpu.make_async_copy(
            inverse.at[0, pl.ds(0, deep), pl.ds(j * width, width)],
            held.at[pl.ds(0, deep), pl.ds(j * width, width)],
            sems.at[j],
        ).wait()
        out[:, j * width : deep] = jnp.dot(
            panel[0, :, :deep], held[:deep, j * width : deep], preferred_element_type=F32
        ).astype(BF)


def factor(panel, inverse):
    vmem = pl.BlockSpec(memory_space=pltpu.VMEM)
    return pl.pallas_call(
        factor_kernel,
        out_shape=jax.ShapeDtypeStruct((OWN, PIV), BF),
        in_specs=[vmem, ANY_SPEC],
        out_specs=vmem,
        scratch_shapes=[pltpu.VMEM((PIV, PIV), BF), pltpu.SemaphoreType.DMA((4,))],
        compiler_params=pltpu.CompilerParams(vmem_limit_bytes=VMEM_LIMIT),
        cost_estimate=pl.CostEstimate(
            flops=2_000_000_000, bytes_accessed=8_000_000, transcendentals=0
        ),
    )(panel, inverse)


def gather_rows(own, ready):
    w = mirrored(own, "x", 1)
    e = mirrored(own, "x", -1)
    z = shift(own, "z", 1)
    core = shift(own, "c", 1)
    w, e, z, core, ready = lax.optimization_barrier((w, e, z, core, ready))
    b = shift(w, "z", 1)
    q = mirrored(w, "x", 1)
    a = mirrored(z, "x", -1)
    cross = [shift(v, "c", 1) for v in (w, e)]
    q, a, b, cross = lax.optimization_barrier((q, a, b, cross))
    r = mirrored(b, "x", 1)
    last = cross + [shift(v, "c", 1) for v in (z, q, a, b, r)]
    pieces, first = [], 0
    for array in (own, w, e, z, q, a, b, r, core, *last):
        pieces.append((array, first, array.shape[0] // BLK))
        first += array.shape[0] // BLK
    return pieces, ready


PLACE = [[0, 3], [2, 5], [4, 7], [1, 6]]


def fetch(ins, pieces, block, dst, sem, first_row=0, count=BLK):
    for ref, (first, blocks) in zip(ins, pieces):

        @pl.when((block >= first) & (block < first + blocks))
        def _(ref=ref, first=first):
            row = pl.multiple_of((block - first) * BLK + first_row, 64)
            pltpu.make_async_copy(ref.at[pl.ds(row, count), :], dst, sem).start()


def fetched(ins, block, dst, sem, count=BLK):
    @pl.when(block < 0)
    def _():
        dst[...] = jnp.zeros((count, PIV), BF)

    @pl.when(block >= 0)
    def _():
        pltpu.make_async_copy(ins[0].at[pl.ds(0, count), :], dst, sem).wait()


def main_kernel(pieces, dest, chosen, *refs):
    n = len(pieces)
    ins, outs = refs[:n], refs[n : n + 16]
    rows, cols, turned, placed, sem_in, sem_sel, sem_out = refs[n + 16 :]

    for m in range(4):
        fetch(ins, pieces, chosen[m], cols.at[pl.ds(m * BLK, BLK), :], sem_sel.at[m])

    def arrival(i):
        first, blocks = pieces[i]
        return pltpu.make_async_copy(
            ins[i], rows.at[pl.ds(first * BLK, blocks * BLK), :], sem_in.at[i]
        )

    early = 4
    for i in range(early):
        arrival(i).start()

    @pl.loop(0, PORD // 256)
    def _(i):
        for half in range(2):
            placed[half, pl.ds(pl.multiple_of(i * 256, 256), 256), :] = jnp.zeros((256, 256), BF)

    for m in range(4):
        fetched(ins, chosen[m], cols.at[pl.ds(m * BLK, BLK), :], sem_sel.at[m])
    for i in range(early, n):
        arrival(i).start()

    turned[...] = cols[...].T

    def multiply(block, count):
        product = jnp.dot(
            rows[pl.ds(block * BLK, count * BLK), :], turned[...], preferred_element_type=F32
        )
        for b in range(count):
            at = pl.multiple_of(dest[block + b] * BLK, BLK)
            result = (-product[b * BLK : (b + 1) * BLK]).astype(BF)
            placed[0, pl.ds(at, BLK), :] = result[:, :256]
            placed[1, pl.ds(at, BLK), :] = result[:, 256:]

    done, at = 0, 0
    for i in range(n):
        arrival(i).wait()
        done += pieces[i][1]
        if (done - at) % STEP == 0:

            @pl.loop(0, (done - at) // STEP)
            def _(k, at=at):
                multiply(at + k * STEP, STEP)

            at = done

    def leaving(i):
        return pltpu.make_async_copy(
            placed.at[i % 2, pl.ds((i // 2) * 1024, 1024), :], outs[i], sem_out.at[i]
        )

    for i in range(16):
        leaving(i).start()
    for i in range(16):
        leaving(i).wait()


def main_parts(pieces, dest, chosen):
    arrays = [p[0] for p in pieces]
    n = len(arrays)
    outs = pl.pallas_call(
        functools.partial(main_kernel, [p[1:] for p in pieces]),
        out_shape=[jax.ShapeDtypeStruct((1024, 256), BF)] * 16,
        in_specs=[SMEM_SPEC] * 2 + [ANY_SPEC] * n,
        out_specs=[ANY_SPEC] * 16,
        scratch_shapes=[
            pltpu.VMEM((6144, PIV), BF),
            pltpu.VMEM((512, PIV), BF),
            pltpu.VMEM((PIV, 512), BF),
            pltpu.VMEM((2, PORD, 256), BF),
            pltpu.SemaphoreType.DMA((n,)),
            pltpu.SemaphoreType.DMA((4,)),
            pltpu.SemaphoreType.DMA((16,)),
        ],
        compiler_params=pltpu.CompilerParams(vmem_limit_bytes=VMEM_LIMIT),
        cost_estimate=pl.CostEstimate(
            flops=20_000_000_000, bytes_accessed=36_000_000, transcendentals=0
        ),
    )(dest, chosen, *arrays)
    return [[[outs[(dh * 4 + dy) * 2 + k] for k in range(2)] for dy in range(4)] for dh in range(2)]


def panel_kernel(pieces, pan_rows, pan_cols, offset, *refs):
    n = len(pieces)
    ins, out = refs[:n], refs[n]
    left, right, sem_left, sem_right = refs[n + 1 :]
    to_left = lambda q: left.at[pl.ds(q * 64, 64), :]
    to_right = lambda q: right.at[pl.ds(q * BLK, BLK), :]
    for q in range(8):
        fetch(ins, pieces, pan_rows[q], to_left(q), sem_left.at[q], offset[0], 64)
        fetch(ins, pieces, pan_cols[q], to_right(q), sem_right.at[q])
    for q in range(8):
        fetched(ins, pan_rows[q], to_left(q), sem_left.at[q], 64)
    for q in range(8):
        fetched(ins, pan_cols[q], to_right(q), sem_right.at[q])

    for part in range(4):
        product = lax.dot_general(
            left[...],
            right[pl.ds(part * 256, 256), :],
            (((1,), (1,)), ((), ())),
            preferred_element_type=F32,
        )
        out[:, part * 256 : (part + 1) * 256] = (-product).astype(BF)


def panel_parts(pieces, pan_rows, pan_cols, offset):
    arrays = [p[0] for p in pieces]
    n = len(arrays)
    return pl.pallas_call(
        functools.partial(panel_kernel, [p[1:] for p in pieces]),
        out_shape=jax.ShapeDtypeStruct((512, 1024), BF),
        in_specs=[SMEM_SPEC] * 3 + [ANY_SPEC] * n,
        out_specs=pl.BlockSpec(memory_space=pltpu.VMEM),
        scratch_shapes=[
            pltpu.VMEM((512, PIV), BF),
            pltpu.VMEM((1024, PIV), BF),
            pltpu.SemaphoreType.DMA((8,)),
            pltpu.SemaphoreType.DMA((8,)),
        ],
        compiler_params=pltpu.CompilerParams(vmem_limit_bytes=VMEM_LIMIT),
        cost_estimate=pl.CostEstimate(
            flops=2_200_000_000, bytes_accessed=8_000_000, transcendentals=0
        ),
    )(pan_rows, pan_cols, offset, *arrays)


class Ring:
    def __init__(self, term, gate=None):
        carried = term(3).astype(BF)
        if gate is not None:
            carried = after(carried, gate)
        self.marks = []
        for k in (2, 1, 0):
            moved = mirrored(carried, "y", 1)
            self.marks.append(moved)
            self.total = term(k).astype(F32) + moved.astype(F32)
            carried = self.total.astype(BF)


def pick(bit, when_zero, when_one):
    return jnp.where(bit == 0, when_zero, when_one)


def ordered_pair(bit, own, other):
    return jnp.stack([pick(bit, own, other), pick(bit, other, own)])


def ordered_ring(at, parts):
    twice = jnp.stack(list(parts) + list(parts))
    return lax.dynamic_slice_in_dim(twice, (4 - at) % 4, 4, 0)


def front_kernel(pivots, place, front, keep, send, zeros, sems):
    zeros[...] = jnp.zeros_like(zeros)
    for r in range(8):
        columns = pl.ds(r * BLK, BLK)
        local_block = pivots[r] - place[0] * 4
        mine = (local_block >= 0) & (local_block < 4)
        for k, out in enumerate((keep, send)):

            @pl.when(mine)
            def _(k=k, out=out, columns=columns, r=r):
                pltpu.make_async_copy(
                    front.at[:, place[1] ^ k, :, pl.ds(pl.multiple_of(local_block * BLK, BLK), BLK)],
                    out.at[:, :, columns],
                    sems.at[r, k],
                ).start()

            @pl.when(jnp.logical_not(mine))
            def _(k=k, out=out, columns=columns, r=r):
                pltpu.make_async_copy(zeros, out.at[:, :, columns], sems.at[r, k]).start()

    for r in range(8):
        for k, out in enumerate((keep, send)):
            pltpu.make_async_copy(zeros, out.at[:, :, pl.ds(r * BLK, BLK)], sems.at[r, k]).wait()


def front_pick(pivots, place, front):
    return pl.pallas_call(
        front_kernel,
        out_shape=[jax.ShapeDtypeStruct((8, 64, 1024), BF)] * 2,
        in_specs=[SMEM_SPEC] * 2 + [ANY_SPEC],
        out_specs=[ANY_SPEC] * 2,
        scratch_shapes=[pltpu.VMEM((8, 64, BLK), BF), pltpu.SemaphoreType.DMA((8, 2))],
        compiler_params=pltpu.CompilerParams(vmem_limit_bytes=VMEM_LIMIT),
    )(pivots, place, front.reshape(8, 2, 64, 512))


def local(child_panel, child_inverse, child_map, parent_front, parent_inverse, parent_pivots):
    h, y, x, z, c = (lax.axis_index(a) for a in AXES)
    sec = h * 4 + y
    dev = x * 4 + z * 2 + c

    my_map = lax.dynamic_index_in_dim(child_map, sec, 0, keepdims=False)
    place_table = jnp.array(PLACE, jnp.int32)
    child = jnp.arange(48, dtype=jnp.int32)
    owner = child // 3
    place = place_table[
        (owner // 4 - x) * (1 - 2 * (owner % 2)) % 4, (owner // 2 % 2) ^ z
    ]
    position = ((owner % 2) ^ c) * 24 + place * 3 + child % 3
    parent_row = my_map // 8
    slot = (((parent_row // 4) ^ h) * 4 + (parent_row % 4 - y) * (1 - 2 * c) % 4) * 8 + my_map % 8
    dest = jnp.sum(
        jnp.where(position[None, :] == child[:, None], slot[None, :], 0), axis=1, dtype=jnp.int32
    )

    def find(targets):
        hit = my_map[None, :] == targets[:, None]
        return jnp.sum(jnp.where(hit, position[None, :] + 1, 0), axis=1, dtype=jnp.int32) - 1

    chosen = find(dev * 4 + jnp.arange(4, dtype=jnp.int32))
    pan_rows = find(jnp.arange(8, dtype=jnp.int32) * 8 + dev // 2)
    pan_cols = find(parent_pivots)
    offset = (dev % 2 * 64).astype(jnp.int32).reshape(1)

    keep, send = front_pick(parent_pivots, jnp.stack([dev, c]).astype(jnp.int32), parent_front)
    front = (keep + shift(send, "c", 1)).reshape(4, 2, 64, 1024)
    front_x = [lax.dynamic_index_in_dim(front, (x + k) % 4, 0, keepdims=False) for k in range(4)]

    pieces, ready = gather_rows(
        factor(child_panel, child_inverse), (dest, chosen, pan_rows, pan_cols, offset, front_x)
    )
    dest, chosen, pan_rows, pan_cols, offset, front_x = ready

    pan = panel_parts(pieces, pan_rows, pan_cols, offset)
    arrived = lax.all_to_all(
        pan.reshape(8, 64, 1024), ("h", "y"), split_axis=0, concat_axis=0, tiled=True
    )
    main = main_parts(pieces, dest, chosen)

    front_x = [after(v, pan) for v in front_x]
    front_z = (
        front_x[0]
        + shift(front_x[1], "x", 1)
        + shift(front_x[3], "x", -1)
        + shift(front_x[2], "x", 2)
    )
    front_rows = pick(z, front_z[0], front_z[1]) + shift(pick(z, front_z[1], front_z[0]), "z", 1)

    arrived, main = lax.optimization_barrier((arrived, main))
    pan_rows_f = arrived.astype(F32).sum(axis=0) + front_rows.astype(F32)
    share = jnp.dot(pan_rows_f.astype(BF), parent_inverse, preferred_element_type=F32).astype(BF)

    rings = []
    for d in (1, 0):
        for half in range(2):
            rings.append(
                Ring(
                    lambda k: main[d][k][half],
                    None if d == 1 else rings[half].marks[0],
                )
            )
    far = [shift(ring.total.astype(BF), "h", 1).astype(F32) for ring in rings[:2]]
    near = jnp.concatenate([rings[2].total + far[0], rings[3].total + far[1]], axis=1)
    assembled = parent_front.astype(F32) + near

    row_block = sec * 8 + dev // 2
    masked = jnp.where(jnp.any(parent_pivots == row_block), jnp.zeros_like(share), share)
    masked = after(masked, rings[0].marks[0])
    pairs = [(s * 16 + d, (d % 8) * 16 + 2 * s + d // 8) for s in range(8) for d in range(16)]
    moved = lax.ppermute(masked, AXES, pairs)
    both = ordered_pair(h, moved, shift(moved, "h", 1))
    both_z = after(ordered_pair(z, share, shift(share, "z", 1)), both)
    both = after(both, rings[1].marks[1])
    ring = ordered_ring(y, [both, shift(both, "y", -1), shift(both, "y", 2), shift(both, "y", 1)])
    column_factor = ring.transpose(1, 0, 2, 3).reshape(512, 1024)

    copies = jnp.broadcast_to(both_z, (8, 2, 64, 1024))
    copies = lax.all_to_all(copies, ("x", "c"), split_axis=0, concat_axis=0, tiled=True)
    parent_factor = copies.reshape(4, 2, 2, 64, 1024).transpose(0, 2, 1, 3, 4).reshape(1024, 1024)

    my_blocks = sec * 8 + jnp.arange(8, dtype=jnp.int32)
    is_pivot = jnp.any(parent_pivots[None, :] == my_blocks[:, None], axis=1)
    row_pivot = jnp.repeat(is_pivot, BLK)
    trailing = jnp.where(row_pivot[:, None], jnp.zeros_like(parent_factor), parent_factor)
    update = lax.dot_general(
        trailing, column_factor, (((1,), (1,)), ((), ())), preferred_element_type=F32
    )
    update = lax.optimization_barrier(update)
    parent_factor = jnp.where(parent_pivots[0] < 0, jnp.zeros_like(parent_factor), parent_factor)
    return assembled - update, parent_factor


def solution(mesh):
    fine = Mesh(mesh.devices.reshape(tuple(SIZE[a] for a in AXES)), AXES)
    sec, dev = ("h", "y"), ("x", "z", "c")
    placed = (P(sec, dev, None), P(sec, None, None), P(), P(sec, dev), P(), P())
    return jax.shard_map(
        local,
        mesh=fine,
        in_specs=placed,
        out_specs=(P(sec, dev), P(sec, None)),
        check_vma=False,
    )
```
